256 devices in a mesh: ctx: 8 (over y, core), tp: 32 (over z, x).
Axes of the slice: x: 4, y: 4, z: 8, core: 2. Of those that a mesh axis runs over, the one named last changes fastest.
Arguments:
- query_in: bfloat16 [8192, 8192], P('ctx', 'tp'), may hold values from -6 to 6
- key_in: bfloat16 [8192, 8192], P('ctx', 'tp'), may hold values from -6 to 6
- value_in: bfloat16 [8192, 8192], P('ctx', 'tp'), may hold values from -6 to 6
- short_taps: float32 [3, 7, 8192], P(None, None, 'tp'), may hold values from -2 to 2
- modal_poles: float32 [16, 8192], P(None, 'tp'), may hold values from 0 to 1, as said below
- modal_residues: float32 [16, 8192], P(None, 'tp'), may hold values from -0.5 to 0.5
- out_weight: bfloat16 [8192, 8192], P('tp'), may hold values from -0.0625 to 0.0625
- grad_out: bfloat16 [8192, 8192], P('ctx', 'tp'), may hold values from -6 to 6
Outputs:
- gated: bfloat16 [8192, 8192], P('ctx', 'tp')
- grad_query: bfloat16 [8192, 8192], P('ctx', 'tp')
- grad_key: bfloat16 [8192, 8192], P('ctx', 'tp')
- grad_value: bfloat16 [8192, 8192], P('ctx', 'tp')
The draws below stay inside these ranges and needn't reach their ends.
Inputs may be any that keep to these rules, and one draw needn't show every extreme that they name: `modal_poles`: every pole lies strictly between 0 and 1.
All inputs are finite; a program needn't handle non-finite values.
Results may differ from the reference program's by a relative error of at most 0.0017.
Values may be sent and summed in bfloat16 or wider, within the bound.
No kernel may reach another device: no remote copies, remote signals or barrier semaphores. Data moves between devices by JAX's collectives and lax.ppermute only.
A program may use at most 128 MiB of HBM per device.

```python
import math
import jax
import jax.numpy as jnp
from jax import lax

D = 8192
MODES = 16
TAPS = 7
SEQ = 8192


def pole_rates(key, slow_share):
    key = jax.random.fold_in(key, 7)
    pick_key, slow_key, fast_key = jax.random.split(key, 3)
    shape = (MODES, D)
    slow_rate = jnp.exp(jax.random.uniform(slow_key, shape, jnp.float32, math.log(0.2 / SEQ), math.log(2.0 / SEQ)))
    fast_rate = jnp.exp(jax.random.uniform(fast_key, shape, jnp.float32, math.log(2.0 / SEQ), math.log(1.0 / 30.0)))
    chosen = jnp.where(jax.random.uniform(pick_key, shape) < slow_share, slow_rate, fast_rate)
    return jnp.exp(-chosen)


def draw_modal_poles(key, part):
    share = 0.5
    return pole_rates(key, share).astype(jnp.float32)


def draw_modal_residues(key, part):
    share = 0.5
    poles_drawn = pole_rates(key, share)
    key = jax.random.fold_in(key, 3)
    normal_part = jnp.clip(jax.random.normal(key, (MODES, D), jnp.float32), -4.0, 4.0)
    return (0.35 * normal_part * jnp.sqrt(1.0 - poles_drawn * poles_drawn)).astype(jnp.float32)


def levels(rng, extent, cuts, low, high):
    gain = 1.0
    for position, parts in cuts:
        draws = jax.random.uniform(jax.random.fold_in(jax.random.fold_in(rng, 6), position), (parts,), jnp.float32, low / len(cuts), high / len(cuts))
        gain = gain * jnp.repeat(jnp.exp(draws), extent[position] // parts).reshape((-1,) + (1,) * (len(extent) - 1 - position))
    return gain


def scatter_about(rng, extent, spread, most, cuts=(), kind=jnp.bfloat16):
    entries = spread * jax.random.normal(rng, extent, jnp.float32)
    if cuts:
        entries = entries * levels(rng, extent, cuts, -0.22, 0.18)
    return jnp.clip(entries, -most, most).astype(kind)


def setup_inputs(seed: int = 0) -> dict:
    seeds = jax.random.split(jax.random.key(seed), 9)
    query_in = scatter_about(seeds[0], (SEQ, D), 1.0, 6.0, ((0, 8), (1, 32)))
    key_in = scatter_about(seeds[1], (SEQ, D), 1.0, 6.0, ((0, 8), (1, 32)))
    value_in = scatter_about(seeds[2], (SEQ, D), 1.0, 6.0, ((0, 8), (1, 32)))
    short_taps = scatter_about(seeds[3], (3, TAPS, D), 0.4, 2.0, ((2, 32),), jnp.float32)
    modal_poles = draw_modal_poles(jax.random.fold_in(seeds[8], 71), 0)
    modal_residues = draw_modal_residues(jax.random.fold_in(seeds[8], 71), 0)
    out_weight = scatter_about(seeds[6], (D, D), D ** -0.5, 0.0625, ((0, 32),))
    grad_out = scatter_about(seeds[7], (SEQ, D), 1.0, 6.0, ((0, 8), (1, 32)))
    return {"query_in": query_in, "key_in": key_in, "value_in": value_in, "short_taps": short_taps, "modal_poles": modal_poles, "modal_residues": modal_residues, "out_weight": out_weight, "grad_out": grad_out}


def short_forward(signal, tap_rows):
    tap_count = tap_rows.shape[0]
    padded = jnp.pad(signal, ((tap_count - 1, 0), (0, 0)))
    summed = jnp.zeros_like(signal)
    for tap_index in range(tap_count):
        begin = tap_count - 1 - tap_index
        summed = summed + tap_rows[tap_index][None, :] * padded[begin:begin + SEQ]
    return summed


def short_backward(signal, tap_rows):
    tap_count = tap_rows.shape[0]
    padded = jnp.pad(signal, ((0, tap_count - 1), (0, 0)))
    summed = jnp.zeros_like(signal)
    for tap_index in range(tap_count):
        summed = summed + tap_rows[tap_index][None, :] * padded[tap_index:tap_index + SEQ]
    return summed


def modal_pass(signal, modal_poles, modal_residues, backward):
    def advance(state, row):
        state = modal_poles * state + row[None, :]
        return state, jnp.sum(modal_residues * state, axis=0)

    _, result = lax.scan(advance, jnp.zeros_like(modal_poles), signal, reverse=backward)
    return result


def reference(query_in, key_in, value_in, short_taps, modal_poles, modal_residues, out_weight, grad_out):
    q_short = short_forward(query_in.astype(jnp.float32), short_taps[0])
    k_short = short_forward(key_in.astype(jnp.float32), short_taps[1])
    v_short = short_forward(value_in.astype(jnp.float32), short_taps[2])
    product = k_short * v_short
    long_out = modal_pass(product, modal_poles, modal_residues, False)
    gated = (q_short * long_out).astype(jnp.bfloat16)
    grad_mixed = jnp.dot(grad_out, out_weight.T, preferred_element_type=jnp.float32)
    grad_qs = grad_mixed * long_out
    grad_long = grad_mixed * q_short
    grad_product = modal_pass(grad_long, modal_poles, modal_residues, True)
    grad_ks = grad_product * v_short
    grad_vs = grad_product * k_short
    grad_query = short_backward(grad_qs, short_taps[0]).astype(jnp.bfloat16)
    grad_key = short_backward(grad_ks, short_taps[1]).astype(jnp.bfloat16)
    grad_value = short_backward(grad_vs, short_taps[2]).astype(jnp.bfloat16)
    return (gated, grad_query, grad_key, grad_value)
```

```python
import functools
import jax
import jax.numpy as jnp
from jax import lax
from jax.experimental import pallas as pl
from jax.experimental.pallas import tpu as pltpu
from jax.sharding import Mesh, PartitionSpec as P

LANES = 128
PARTS = 8
RIM = 8
X_COUNT = 4
TILE = 256
HEAD = 16
SPAN = 32768.0
TINY = 1e-30
LEAST = 1e-37
VMEM_LIMIT = 16 * 1024 * 1024


def power(base, exponent):
    result = None
    while exponent:
        if exponent & 1:
            result = base if result is None else result * base
        exponent >>= 1
        if exponent:
            base = base * base
    return result


def rows_of(ref, lanes):
    return [ref[m : m + 1, lanes] for m in range(ref.shape[0])]


def spread(row):
    return jnp.broadcast_to(row, (PARTS, LANES))


def lane_blocks(width):
    return [(n, pl.ds(n * LANES, LANES)) for n in range(width // LANES)]


def short_filters(q_ref, k_ref, v_ref, prior_ref, taps_ref, poles_ref, qs_ref, ks_ref, vs_ref, ends_ref, own_ref, natural):
    tokens, width = q_ref.shape
    tap_count = taps_ref.shape[1]
    modes = poles_ref.shape[0]
    steps = tokens // PARTS
    for which, (source, target) in enumerate(((q_ref, qs_ref), (k_ref, ks_ref), (v_ref, vs_ref))):
        for block, lanes in lane_blocks(width):
            natural[block, 0:RIM, :] = prior_ref[which, :, lanes].astype(jnp.float32)[prior_ref.shape[1] - RIM :]
            natural[block, RIM:, :] = source[:, lanes].astype(jnp.float32)
        for block, lanes in lane_blocks(width):
            taps = [spread(taps_ref[which, j : j + 1, lanes]) for j in range(tap_count)]

            def tap_step(i, window):
                fresh = natural[block, pl.ds(RIM + i, PARTS, stride=steps), :]
                window = (fresh,) + window
                total = taps[0] * window[0]
                for j in range(1, tap_count):
                    total = total + taps[j] * window[j]
                target[pl.ds(pl.multiple_of(i * PARTS, PARTS), PARTS), lanes] = total
                return window[:-1]

            before = tuple(
                natural[block, pl.ds(RIM - 1 - d, PARTS, stride=steps), :] for d in range(tap_count - 1)
            )
            lax.fori_loop(0, steps, tap_step, before, unroll=8)
    for block, lanes in lane_blocks(width):
        poles = [spread(row) for row in rows_of(poles_ref, lanes)]

        def state_step(i, states):
            rows = pl.ds(pl.multiple_of(i * PARTS, PARTS), PARTS)
            fresh = ks_ref[rows, lanes] * vs_ref[rows, lanes]
            return tuple(p * s + fresh for p, s in zip(poles, states))

        zero = jnp.zeros((PARTS, LANES), jnp.float32)
        states = lax.fori_loop(0, steps, state_step, (zero,) * modes, unroll=4)
        for m in range(modes):
            ends_ref[m, :, lanes] = states[m]
    part_decay = power(poles_ref[...], steps)
    own = ends_ref[:, 0, :]
    for c in range(1, PARTS):
        own = part_decay * own + ends_ref[:, c, :]
    own_ref[...] = own


def long_forward(qs_ref, ks_ref, vs_ref, ends_ref, before_ref, poles_ref, residues_ref, long_ref, gated_ref, first, natural):
    tokens, width = qs_ref.shape
    modes = poles_ref.shape[0]
    steps = tokens // PARTS
    part_decay = power(poles_ref[...], steps)
    entering = before_ref[...]
    for c in range(PARTS):
        first[:, c, :] = entering
        if c < PARTS - 1:
            entering = part_decay * entering + ends_ref[:, c, :]
    for block, lanes in lane_blocks(width):
        poles = [spread(row) for row in rows_of(poles_ref, lanes)]
        residues = [spread(row) for row in rows_of(residues_ref, lanes)]

        def step(i, states):
            rows = pl.ds(pl.multiple_of(i * PARTS, PARTS), PARTS)
            fresh = ks_ref[rows, lanes] * vs_ref[rows, lanes]
            states = tuple(p * s + fresh for p, s in zip(poles, states))
            total = mixed(residues, states)
            long_ref[rows, lanes] = total
            natural[block, pl.ds(i, PARTS, stride=steps), :] = total * qs_ref[rows, lanes]
            return states

        lax.fori_loop(0, steps, step, tuple(first[m, :, lanes] for m in range(modes)), unroll=4)
    for block, lanes in lane_blocks(width):
        gated_ref[:, lanes] = natural[block].astype(gated_ref.dtype)


def mixed(residues, states):
    return added([r * s for r, s in zip(residues, states)])


def added(terms):
    while len(terms) > 1:
        terms = [a + b for a, b in zip(terms[::2], terms[1::2])] + list(terms[len(terms) // 2 * 2 :])
    return terms[0]


def back_states(kept_ref, one_ref, three_ref, qs_ref, long_ref, poles_ref, mixed_ref, starts_ref, own_ref, rim_ref, rim_starts, natural):
    tokens, width = qs_ref.shape
    modes = poles_ref.shape[0]
    steps = tokens // PARTS
    for block, lanes in lane_blocks(width):
        poles = [spread(row) for row in rows_of(poles_ref, lanes)]

        def add_step(n, carry):
            piece = 64
            row = pl.multiple_of(n * piece, piece)
            tile, inside = row // TILE, pl.multiple_of(row % TILE, piece)
            total = kept_ref[pl.ds(row, piece), lanes]
            for ref in (one_ref, three_ref):
                start = pl.multiple_of(tile * (TILE + HEAD), HEAD)
                total = total + decoded(ref, start, pl.ds(inside, piece), lanes)
            natural[block, pl.ds(row, piece), :] = total
            return carry

        lax.fori_loop(0, tokens // 64, add_step, 0)

        def step(back, states):
            i = steps - 1 - back
            rows = pl.ds(pl.multiple_of(i * PARTS, PARTS), PARTS)
            here = natural[block, pl.ds(i, PARTS, stride=steps), :]
            mixed_ref[rows, lanes] = here
            fresh = here * qs_ref[rows, lanes]
            return tuple(p * s + fresh for p, s in zip(poles, states))

        zero = jnp.zeros((PARTS, LANES), jnp.float32)
        states = lax.fori_loop(0, steps - RIM, step, (zero,) * modes, unroll=4)
        for m in range(modes):
            rim_starts[m, :, lanes] = states[m]
        states = lax.fori_loop(steps - RIM, steps, step, states, unroll=4)
        for m in range(modes):
            starts_ref[m, :, lanes] = states[m]
    part_decay = power(poles_ref[...], steps)
    own = starts_ref[:, PARTS - 1, :]
    for c in range(PARTS - 2, 0, -1):
        own = part_decay * own + starts_ref[:, c, :]
    own_ref[...] = part_decay * own + starts_ref[:, 0, :]
    rim_ref[0:modes, :] = power(poles_ref[...], steps - RIM) * own + rim_starts[:, 0, :]
    for i in range(RIM):
        here = mixed_ref[i * PARTS : i * PARTS + 1, :]
        rim_ref[modes + i : modes + i + 1, :] = here * qs_ref[i * PARTS : i * PARTS + 1, :]
        rim_ref[modes + RIM + i : modes + RIM + i + 1, :] = here * long_ref[i * PARTS : i * PARTS + 1, :]


def back_local(mixed_ref, qs_ref, poles_ref, residues_ref, local_ref):
    tokens, width = qs_ref.shape
    modes = poles_ref.shape[0]
    steps = tokens // PARTS
    for block, lanes in lane_blocks(width):
        poles = [spread(row) for row in rows_of(poles_ref, lanes)]
        residues = [spread(row) for row in rows_of(residues_ref, lanes)]

        def step(back, states):
            i = steps - 1 - back
            rows = pl.ds(pl.multiple_of(i * PARTS, PARTS), PARTS)
            fresh = mixed_ref[rows, lanes] * qs_ref[rows, lanes]
            states = tuple(p * s + fresh for p, s in zip(poles, states))
            local_ref[rows, lanes] = mixed(residues, states)
            return states

        zero = jnp.zeros((PARTS, LANES), jnp.float32)
        lax.fori_loop(0, steps, step, (zero,) * modes, unroll=4)


def short_back(value, rim, taps_ref, which, target, natural):
    tokens, width = target.shape
    tap_count = taps_ref.shape[1]
    steps = tokens // PARTS
    bottom = lax.broadcasted_iota(jnp.int32, (PARTS, LANES), 0) == PARTS - 1
    for block, lanes in lane_blocks(width):
        taps = [spread(taps_ref[which, j : j + 1, lanes]) for j in range(tap_count)]

        def tap_step(back, window):
            i = steps - 1 - back
            window = (value(pl.ds(pl.multiple_of(i * PARTS, PARTS), PARTS), lanes),) + window
            total = taps[0] * window[0]
            for j in range(1, tap_count):
                total = total + taps[j] * window[j]
            natural[block, pl.ds(i, PARTS, stride=steps), :] = total
            return window[:-1]

        after = tuple(
            jnp.where(
                bottom,
                spread(rim(d, lanes)),
                pltpu.roll(value(pl.ds(d * PARTS, PARTS), lanes), PARTS - 1, 0),
            )
            for d in range(tap_count - 1)
        )
        lax.fori_loop(0, steps, tap_step, after, unroll=8)
    for block, lanes in lane_blocks(width):
        target[:, lanes] = natural[block].astype(target.dtype)


def back_query(mixed_ref, long_ref, next_ref, taps_ref, gq_ref, natural):
    first = next_ref.shape[0] - RIM
    short_back(
        lambda rows, lanes: mixed_ref[rows, lanes] * long_ref[rows, lanes],
        lambda d, lanes: next_ref[first + d : first + d + 1, lanes],
        taps_ref, 0, gq_ref, natural,
    )


def back_filters(local_ref, ks_ref, vs_ref, starts_ref, next_ref, beyond_ref, next_kv_ref, taps_ref, poles_ref, residues_ref, gk_ref, gv_ref, last, product, natural, rims):
    tokens, width = ks_ref.shape
    modes = poles_ref.shape[0]
    steps = tokens // PARTS
    poles_all = poles_ref[...]
    residues_all = residues_ref[...]
    entering = next_ref[0:modes, :] + power(poles_all, tokens - RIM) * beyond_ref[...]
    for i in range(RIM - 1, -1, -1):
        entering = poles_all * entering + next_ref[modes + i : modes + i + 1, :]
        here = jnp.sum(residues_all * entering, axis=0, keepdims=True)
        rims[0, i : i + 1, :] = here * next_kv_ref[1, i : i + 1, :]
        rims[1, i : i + 1, :] = here * next_kv_ref[0, i : i + 1, :]
    part_decay = power(poles_all, steps)
    for c in range(PARTS - 1, -1, -1):
        last[:, c, :] = residues_all * entering
        if c:
            entering = part_decay * entering + starts_ref[:, c, :]
    for block, lanes in lane_blocks(width):
        poles = [spread(row) for row in rows_of(poles_ref, lanes)]

        def step(back, fading):
            i = steps - 1 - back
            rows = pl.ds(pl.multiple_of(i * PARTS, PARTS), PARTS)
            fading = tuple(p * s for p, s in zip(poles, fading))
            product[rows, lanes] = local_ref[rows, lanes] + added(fading)
            return fading

        lax.fori_loop(0, steps, step, tuple(last[m, :, lanes] for m in range(modes)), unroll=4)
    for which, other, target in ((1, vs_ref, gk_ref), (2, ks_ref, gv_ref)):
        short_back(
            lambda rows, lanes: product[rows, lanes] * other[rows, lanes],
            lambda d, lanes: rims[which - 1, d : d + 1, lanes],
            taps_ref, which, target, natural,
        )


def pick_shares(place_ref, weight_ref, up_ref, down_ref, arrived):
    rows = weight_ref.shape[0] // 2
    blocks = arrived.shape[2]
    depth = up_ref.shape[1]
    width = depth // blocks
    count = weight_ref.shape[1] // depth
    first = pl.multiple_of(place_ref[2] * rows, rows)
    copies = []
    for side, (message_ref, step) in enumerate(((up_ref, 1), (down_ref, count - 1))):
        for part, (x, begin, size, target) in enumerate(
            (
                (lax.rem(place_ref[0] + step, count), 0, rows, 0),
                (lax.rem(place_ref[0] + 2, count), side * (rows // 2), rows // 2, rows),
            )
        ):
            for z in range(blocks):
                column = pl.multiple_of((z * count + x) * width, width)
                copies.append(
                    pltpu.make_async_copy(
                        weight_ref.at[pl.ds(first + begin, size), pl.ds(column, width)],
                        message_ref.at[pl.ds(target, size), pl.ds(z * width, width)],
                        arrived.at[side, part, z],
                    )
                )
    for copy in copies:
        copy.start()
    for copy in copies:
        copy.wait()


def join_shares(place_ref, share_ref, other_ref, j, weight):
    rows = share_ref.shape[1]
    core = place_ref[2]
    weight[pl.ds(pl.multiple_of(core * rows, rows), rows), :] = share_ref[j]
    weight[pl.ds(pl.multiple_of((1 - core) * rows, rows), rows), :] = other_ref[j]


def ring_product(target_ref, ring, weight_ref, column_of):
    tokens, width = target_ref.shape
    rows = tokens // 2
    first = True
    for n, refs in ring:
        for half in range(2):
            target_rows = pl.ds(half * rows, rows)
            features = refs[half][...] if len(refs) == 2 else refs[0][target_rows, :]
            term = lax.dot_general(
                features,
                weight_ref[:, pl.ds(column_of(n), width)],
                (((1,), (1,)), ((), ())),
                preferred_element_type=jnp.float32,
            )
            target_ref[target_rows, :] = term if first else target_ref[target_rows, :] + term
        first = False


def in_places(early_ref, left_ref, right_ref, *middle):
    count = early_ref.shape[0] + 3
    ring = [(n % count, (early_ref.at[n + 2],)) for n in range(-2, 3)]
    ring += [(3, (left_ref,)), (count - 3, (right_ref,))]
    return ring + [(count // 2, middle)] if middle else ring


def collect(*refs):
    *block_refs, early_ref, arrived = refs
    copies = [
        pltpu.make_async_copy(ref, early_ref.at[n], arrived.at[n]) for n, ref in enumerate(block_refs)
    ]
    for copy in copies:
        copy.start()
    for copy in copies:
        copy.wait()


def encode_tile(total, coded_ref, tile):
    largest = jnp.max(jnp.abs(total), axis=0, keepdims=True) * 1.01
    largest = jnp.maximum(largest, TINY).astype(jnp.bfloat16)
    scaled = total * (SPAN / largest.astype(jnp.float32))
    square = scaled * scaled
    fourth = square * square
    eighth = fourth * fourth
    code = jnp.where(scaled < 0, -eighth, eighth)
    start = pl.multiple_of(tile * (TILE + HEAD), HEAD)
    coded_ref[pl.ds(start, HEAD), :] = jnp.broadcast_to(largest, (HEAD, largest.shape[1]))
    coded_ref[pl.ds(start + HEAD, TILE), :] = code.astype(jnp.bfloat16)


def column_on_ring(place_ref, count, width):
    return lambda n: pl.multiple_of(lax.rem(place_ref[3] + n, count) * width, width)


def far_start(place_ref, *refs):
    *ring_refs, shares_ref, other_ref, far_ref, weight = refs
    width = far_ref.shape[1]
    join_shares(place_ref, shares_ref, other_ref, 1, weight)
    column_of = column_on_ring(place_ref, weight.shape[1] // width, width)
    ring_product(far_ref, in_places(*ring_refs), weight, column_of)


def far_finish(place_ref, far_ref, middle_up_ref, middle_down_ref, shares_ref, other_ref, up_ref, down_ref, weight):
    half, width = middle_up_ref.shape
    count = weight.shape[1] // width
    join_shares(place_ref, shares_ref, other_ref, 1, weight)
    column = column_on_ring(place_ref, count, width)(count // 2)
    for side, (features_ref, coded_ref) in enumerate(((middle_up_ref, up_ref), (middle_down_ref, down_ref))):

        def tile_step(t, carry):
            row = pl.multiple_of(t * TILE, TILE)
            term = lax.dot_general(
                features_ref[pl.ds(row, TILE), :],
                weight[:, pl.ds(column, width)],
                (((1,), (1,)), ((), ())),
                preferred_element_type=jnp.float32,
            )
            encode_tile(far_ref[pl.ds(pl.multiple_of(side * half + row, TILE), TILE), :] + term, coded_ref, t)
            return carry

        lax.fori_loop(0, half // TILE, tile_step, 0)


def near_products(place_ref, *refs):
    *ring_refs, shares_ref, other_ref, next_ref, last_ref, weight = refs
    width = next_ref.shape[1]
    column_of = column_on_ring(place_ref, weight.shape[1] // width, width)
    for j, target in ((0, next_ref), (2, last_ref)):
        join_shares(place_ref, shares_ref, other_ref, j, weight)
        ring_product(target, in_places(*ring_refs), weight, column_of)


def keep_product(place_ref, *refs):
    *ring_refs, weight_ref, kept_ref = refs
    width = kept_ref.shape[1]
    count = ring_refs[0].shape[0] + 3
    along_x = weight_ref.shape[1] // (count * width)

    def column_of(n):
        block = lax.rem(place_ref[3] + n, count) * along_x + place_ref[0]
        return pl.multiple_of(block * width, width)

    ring_product(kept_ref, in_places(*ring_refs), weight_ref, column_of)


def send_near(next_ref, last_ref, up_ref, down_ref, next_coded_ref, last_coded_ref):
    tokens, width = next_ref.shape
    tiles = tokens // TILE
    half = tiles // 2
    everything = pl.ds(0, width)

    for t in range(tiles):
        rows = pl.ds(t * TILE, TILE)
        start = t % half * (TILE + HEAD)
        after, before = next_ref[rows, :], last_ref[rows, :]
        if t < half:
            after = after + decoded(up_ref, start, pl.ds(0, TILE), everything)
        else:
            before = before + decoded(down_ref, start, pl.ds(0, TILE), everything)
        encode_tile(after, next_coded_ref, t)
        encode_tile(before, last_coded_ref, t)


def decoded(coded_ref, start, rows, lanes):
    largest = coded_ref[pl.ds(start, HEAD), lanes].astype(jnp.float32)[0:1]
    code = coded_ref[pl.ds(start + HEAD + rows.start, rows.size), lanes].astype(jnp.float32)
    size = jnp.exp2(jnp.log2(jnp.maximum(jnp.abs(code), LEAST)) * 0.125)
    value = jnp.where(code < 0, -size, size) * (largest * (1.0 / SPAN))
    return jnp.where(code == 0, 0.0, value)


def local_call(kernel, outs, scratch, operands, cost):
    whole = pl.BlockSpec(memory_space=pltpu.VMEM)
    return pl.pallas_call(
        kernel,
        out_shape=outs,
        in_specs=[whole if o.ndim > 1 else pl.BlockSpec(memory_space=pltpu.SMEM) for o in operands],
        out_specs=[whole] * len(outs),
        scratch_shapes=scratch,
        compiler_params=pltpu.CompilerParams(vmem_limit_bytes=VMEM_LIMIT),
        cost_estimate=pl.CostEstimate(flops=cost, bytes_accessed=cost // 64, transcendentals=0),
    )(*operands)


def floats(*shape):
    return jax.ShapeDtypeStruct(shape, jnp.float32)


def shift(block, axis, distance, size):
    return lax.ppermute(block, axis, [(i, (i + distance) % size) for i in range(size)])


def from_behind(block, axis, distance, size):
    return lax.ppermute(
        block, axis, [(i - distance, i) for i in range(size) if 0 <= i - distance < size]
    )


def shards(
    sizes, query_in, key_in, value_in, short_taps, modal_poles, modal_residues, out_weight, grad_out
):
    ctx_count, z_count, x_count = sizes
    tokens, width = query_in.shape
    modes = modal_poles.shape[0]
    slab = floats(tokens, width)
    rounded = jax.ShapeDtypeStruct((tokens, width), jnp.bfloat16)
    per_part = floats(modes, PARTS, width)
    state = floats(modes, width)
    slab_scratch = pltpu.VMEM((tokens, width), jnp.float32)
    natural_scratch = pltpu.VMEM((width // LANES, tokens, LANES), jnp.float32)
    part_scratch = pltpu.VMEM((modes, PARTS, width), jnp.float32)
    together = lax.optimization_barrier
    decay_1 = power(modal_poles, tokens)
    decay_2 = decay_1 * decay_1

    ctx = lax.axis_index("ctx")
    place = jnp.stack([lax.axis_index("x"), ctx // 2, ctx % 2, lax.axis_index("z")])

    right_1 = shift(grad_out, "z", 1, z_count)
    left_1 = shift(grad_out, "z", -1, z_count)
    tails = jnp.stack([a[tokens - 16 :] for a in (query_in, key_in, value_in)])
    prior = from_behind(tails, "ctx", 1, ctx_count)
    place, prior = together((place, prior))
    message = jax.ShapeDtypeStruct((width // 4 * 3, z_count * width), jnp.bfloat16)
    up, down = pl.pallas_call(
        pick_shares,
        out_shape=[message] * 2,
        in_specs=[pl.BlockSpec(memory_space=pltpu.SMEM), pl.BlockSpec(memory_space=pltpu.HBM)],
        out_specs=[pl.BlockSpec(memory_space=pltpu.VMEM)] * 2,
        scratch_shapes=[pltpu.SemaphoreType.DMA((2, 2, z_count))],
        compiler_params=pltpu.CompilerParams(vmem_limit_bytes=VMEM_LIMIT),
    )(place, out_weight)
    up = shift(up, "x", 1, x_count)
    down = shift(down, "x", -1, x_count)
    q_short, k_short, v_short, ends, own_end = local_call(
        short_filters,
        [slab, slab, slab, per_part, state],
        [pltpu.VMEM((width // LANES, tokens + RIM, LANES), jnp.float32)],
        (query_in, key_in, value_in, prior, short_taps, modal_poles),
        tokens * width * 80,
    )
    right_2 = shift(right_1, "z", 1, z_count)
    left_2 = shift(left_1, "z", -1, z_count)
    one = from_behind(own_end, "ctx", 1, ctx_count)
    right_2, left_2, one, up, down = together((right_2, left_2, one, up, down))

    right_3 = shift(right_2, "z", 1, z_count)
    left_3 = shift(left_2, "z", -1, z_count)
    rows = width // 2
    far_up = shift(up[rows:], "x", 1, x_count)
    far_down = shift(down[rows:], "x", -1, x_count)
    anywhere = pl.BlockSpec(memory_space=pl.ANY)
    blocks = (right_2, right_1, grad_out, left_1, left_2)
    early = pl.pallas_call(
        collect,
        out_shape=jax.ShapeDtypeStruct((len(blocks), tokens, width), jnp.bfloat16),
        in_specs=[anywhere] * len(blocks),
        out_specs=pl.BlockSpec(memory_space=pltpu.VMEM),
        scratch_shapes=[pltpu.SemaphoreType.DMA((len(blocks),))],
        compiler_params=pltpu.CompilerParams(vmem_limit_bytes=VMEM_LIMIT),
    )(*blocks)
    right_3, left_3, far_up, far_down, early = together((right_3, left_3, far_up, far_down, early))

    middle_up = shift(right_3[: tokens // 2], "z", 1, z_count)
    middle_down = shift(left_3[tokens // 2 :], "z", -1, z_count)
    shares = jnp.stack([down[:rows], jnp.concatenate([far_up, far_down]), up[:rows]])
    other = lax.ppermute(shares, "ctx", [(i, i ^ 1) for i in range(ctx_count)])

    weight_scratch = pltpu.VMEM((width, z_count * width), jnp.bfloat16)
    product_cost = tokens * width * z_count * width * 2
    half_code = jax.ShapeDtypeStruct((tokens // TILE // 2 * (TILE + HEAD), width), jnp.bfloat16)
    code = jax.ShapeDtypeStruct((tokens // TILE * (TILE + HEAD), width), jnp.bfloat16)
    (far,) = local_call(
        far_start,
        [slab],
        [weight_scratch],
        (place, early, left_3, right_3, shares, other),
        product_cost,
    )
    middle_up, middle_down, far = together((middle_up, middle_down, far))
    on_ring = (early, left_3, right_3, middle_up, middle_down)
    up, down = local_call(
        far_finish,
        [half_code, half_code],
        [weight_scratch],
        (place, far, middle_up, middle_down, shares, other),
        product_cost // z_count,
    )
    up = shift(up, "x", 1, x_count)
    down = shift(down, "x", -1, x_count)
    after, last = local_call(
        near_products,
        [slab, slab],
        [weight_scratch],
        (place, *on_ring, shares, other),
        2 * product_cost,
    )
    pair = own_end + decay_1 * one
    two = from_behind(pair, "ctx", 2, ctx_count)
    up, down, after, last, two = together((up, down, after, last, two))
    after, last = local_call(
        send_near, [code, code], [], (after, last, up, down), tokens * width * 64
    )
    after = shift(after, "x", 1, x_count)
    last = shift(last, "x", -1, x_count)
    four = from_behind(pair + decay_2 * two, "ctx", 4, ctx_count)
    before = one + decay_1 * two + decay_2 * decay_1 * four
    first_kv = jnp.stack([k_short[: RIM * PARTS : PARTS], v_short[: RIM * PARTS : PARTS]])
    next_kv = from_behind(first_kv, "ctx", -1, ctx_count)
    (kept,) = local_call(
        keep_product, [slab], [], (place, *on_ring, out_weight), product_cost
    )
    long_out, gated = local_call(
        long_forward,
        [slab, rounded],
        [part_scratch, natural_scratch],
        (q_short, k_short, v_short, ends, before, modal_poles, modal_residues),
        tokens * width * 70,
    )
    after, last, gated, kept, next_kv = together((after, last, gated, kept, next_kv))
    mixed_steps, starts, own_start, rim = local_call(
        back_states,
        [slab, per_part, state, floats(modes + 2 * RIM, width)],
        [part_scratch, natural_scratch],
        (kept, after, last, q_short, long_out, modal_poles),
        tokens * width * 40,
    )

    near = from_behind(jnp.concatenate([rim, own_start]), "ctx", -1, ctx_count)
    (local,) = local_call(
        back_local, [slab], [], (mixed_steps, q_short, modal_poles, modal_residues), tokens * width * 64
    )
    two = from_behind(own_start, "ctx", -2, ctx_count)
    near, two, local = together((near, two, local))
    rim_size = modes + 2 * RIM
    near_rim = near[:rim_size]
    triple = own_start + decay_1 * near[rim_size:] + decay_2 * two
    triple_2 = from_behind(triple, "ctx", -2, ctx_count)
    triple_5 = from_behind(triple, "ctx", -5, ctx_count)
    (grad_query,) = local_call(
        back_query,
        [rounded],
        [natural_scratch],
        (mixed_steps, long_out, near_rim, short_taps),
        tokens * width * 20,
    )
    triple_2, triple_5, grad_query = together((triple_2, triple_5, grad_query))
    beyond = triple_2 + decay_2 * decay_1 * triple_5
    grad_key, grad_value = local_call(
        back_filters,
        [rounded, rounded],
        [part_scratch, slab_scratch, natural_scratch, pltpu.VMEM((2, RIM, width), jnp.float32)],
        (
            local, k_short, v_short, starts, near_rim, beyond, next_kv,
            short_taps, modal_poles, modal_residues,
        ),
        tokens * width * 80,
    )
    return gated, grad_query, grad_key, grad_value


def solution(mesh):
    ctx_count, tp_count = mesh.shape["ctx"], mesh.shape["tp"]
    sizes = (ctx_count, tp_count // X_COUNT, X_COUNT)
    grid = Mesh(mesh.devices.reshape(sizes), ("ctx", "z", "x"))
    tp = ("z", "x")
    placed = (
        P("ctx", tp),
        P("ctx", tp),
        P("ctx", tp),
        P(None, None, tp),
        P(None, tp),
        P(None, tp),
        P(tp, None),
        P("ctx", tp),
    )
    return jax.shard_map(
        functools.partial(shards, sizes),
        mesh=grid,
        in_specs=placed,
        out_specs=(P("ctx", tp),) * 4,
        check_vma=False,
    )
```

```python
import functools
import jax
import jax.numpy as jnp
from jax import lax
from jax.experimental import pallas as pl
from jax.experimental.pallas import tpu as pltpu
from jax.sharding import Mesh, PartitionSpec as P

LANES = 128
PARTS = 8
RIM = 8
X_COUNT = 4
RING = 8
TILE = 256
HEAD = 16
SPAN = 32768.0
TINY = 1e-30
LEAST = 1e-37
VMEM_LIMIT = 16 * 1024 * 1024


def power(base, exponent):
    result = None
    while exponent:
        if exponent & 1:
            result = base if result is None else result * base
        exponent >>= 1
        if exponent:
            base = base * base
    return result


def rows_of(ref, lanes):
    return [ref[m : m + 1, lanes] for m in range(ref.shape[0])]


def spread(row):
    return jnp.broadcast_to(row, (PARTS, LANES))


def lane_blocks(width):
    return [(n, pl.ds(n * LANES, LANES)) for n in range(width // LANES)]


def short_filters(q_ref, k_ref, v_ref, prior_ref, taps_ref, poles_ref, qs_ref, ks_ref, vs_ref, ends_ref, own_ref, first_ref, natural):
    tokens, width = q_ref.shape
    tap_count = taps_ref.shape[1]
    modes = poles_ref.shape[0]
    steps = tokens // PARTS
    for which, (source, target) in enumerate(((q_ref, qs_ref), (k_ref, ks_ref), (v_ref, vs_ref))):
        for block, lanes in lane_blocks(width):
            natural[block, 0:RIM, :] = prior_ref[which, :, lanes].astype(jnp.float32)[prior_ref.shape[1] - RIM :]
            natural[block, RIM:, :] = source[:, lanes].astype(jnp.float32)
        for block, lanes in lane_blocks(width):
            taps = [spread(taps_ref[which, j : j + 1, lanes]) for j in range(tap_count)]

            def tap_step(i, window):
                fresh = natural[block, pl.ds(RIM + i, PARTS, stride=steps), :]
                window = (fresh,) + window
                total = taps[0] * window[0]
                for j in range(1, tap_count):
                    total = total + taps[j] * window[j]
                target[pl.ds(pl.multiple_of(i * PARTS, PARTS), PARTS), lanes] = total
                return window[:-1]

            before = tuple(
                natural[block, pl.ds(RIM - 1 - d, PARTS, stride=steps), :] for d in range(tap_count - 1)
            )
            lax.fori_loop(0, steps, tap_step, before, unroll=8)
    for block, lanes in lane_blocks(width):
        poles = [spread(row) for row in rows_of(poles_ref, lanes)]

        def state_step(i, states):
            rows = pl.ds(pl.multiple_of(i * PARTS, PARTS), PARTS)
            fresh = ks_ref[rows, lanes] * vs_ref[rows, lanes]
            return tuple(p * s + fresh for p, s in zip(poles, states))

        zero = jnp.zeros((PARTS, LANES), jnp.float32)
        states = lax.fori_loop(0, steps, state_step, (zero,) * modes, unroll=4)
        for m in range(modes):
            ends_ref[m, :, lanes] = states[m]
    part_decay = power(poles_ref[...], steps)
    own = ends_ref[:, 0, :]
    for c in range(1, PARTS):
        own = part_decay * own + ends_ref[:, c, :]
    own_ref[...] = own
    for i in range(RIM):
        first_ref[0, i : i + 1, :] = ks_ref[i * PARTS : i * PARTS + 1, :]
        first_ref[1, i : i + 1, :] = vs_ref[i * PARTS : i * PARTS + 1, :]


def long_forward(qs_ref, ks_ref, vs_ref, ends_ref, before_ref, poles_ref, residues_ref, long_ref, gated_ref, first, natural):
    tokens, width = qs_ref.shape
    modes = poles_ref.shape[0]
    steps = tokens // PARTS
    part_decay = power(poles_ref[...], steps)
    entering = before_ref[...]
    for c in range(PARTS):
        first[:, c, :] = entering
        if c < PARTS - 1:
            entering = part_decay * entering + ends_ref[:, c, :]
    for block, lanes in lane_blocks(width):
        poles = [spread(row) for row in rows_of(poles_ref, lanes)]
        residues = [spread(row) for row in rows_of(residues_ref, lanes)]

        def step(i, states):
            rows = pl.ds(pl.multiple_of(i * PARTS, PARTS), PARTS)
            fresh = ks_ref[rows, lanes] * vs_ref[rows, lanes]
            states = tuple(p * s + fresh for p, s in zip(poles, states))
            total = mixed(residues, states)
            long_ref[rows, lanes] = total
            natural[block, pl.ds(i, PARTS, stride=steps), :] = total * qs_ref[rows, lanes]
            return states

        lax.fori_loop(0, steps, step, tuple(first[m, :, lanes] for m in range(modes)), unroll=4)
    for block, lanes in lane_blocks(width):
        gated_ref[:, lanes] = natural[block].astype(gated_ref.dtype)


def mixed(residues, states):
    return added([r * s for r, s in zip(residues, states)])


def added(terms):
    while len(terms) > 1:
        terms = [a + b for a, b in zip(terms[::2], terms[1::2])] + list(terms[len(terms) // 2 * 2 :])
    return terms[0]


def back_states(kept_ref, one_up_ref, one_down_ref, three_up_ref, three_down_ref, qs_ref, long_ref, poles_ref, mixed_ref, starts_ref, own_ref, rim_ref, rim_starts, natural):
    tokens, width = qs_ref.shape
    modes = poles_ref.shape[0]
    steps = tokens // PARTS
    for block, lanes in lane_blocks(width):
        poles = [spread(row) for row in rows_of(poles_ref, lanes)]

        for half, refs in enumerate(((one_up_ref, three_up_ref), (one_down_ref, three_down_ref))):

            def add_step(n, carry):
                piece = 64
                row = pl.multiple_of(n * piece, piece)
                tile, inside = row // TILE, pl.multiple_of(row % TILE, piece)
                there = pl.ds(pl.multiple_of(half * (tokens // 2) + row, piece), piece)
                total = kept_ref[there, lanes]
                for ref in refs:
                    start = pl.multiple_of(tile * (TILE + HEAD), HEAD)
                    total = total + decoded(ref, start, pl.ds(inside, piece), lanes)
                natural[block, there, :] = total
                return carry

            lax.fori_loop(0, tokens // 128, add_step, 0)

        def step(back, states):
            i = steps - 1 - back
            rows = pl.ds(pl.multiple_of(i * PARTS, PARTS), PARTS)
            here = natural[block, pl.ds(i, PARTS, stride=steps), :]
            mixed_ref[rows, lanes] = here
            fresh = here * qs_ref[rows, lanes]
            return tuple(p * s + fresh for p, s in zip(poles, states))

        zero = jnp.zeros((PARTS, LANES), jnp.float32)
        states = lax.fori_loop(0, steps - RIM, step, (zero,) * modes, unroll=4)
        for m in range(modes):
            rim_starts[m, :, lanes] = states[m]
        states = lax.fori_loop(steps - RIM, steps, step, states, unroll=4)
        for m in range(modes):
            starts_ref[m, :, lanes] = states[m]
    part_decay = power(poles_ref[...], steps)
    own = starts_ref[:, PARTS - 1, :]
    for c in range(PARTS - 2, 0, -1):
        own = part_decay * own + starts_ref[:, c, :]
    own_ref[...] = part_decay * own + starts_ref[:, 0, :]
    rim_ref[0:modes, :] = power(poles_ref[...], steps - RIM) * own + rim_starts[:, 0, :]
    for i in range(RIM):
        here = mixed_ref[i * PARTS : i * PARTS + 1, :]
        rim_ref[modes + i : modes + i + 1, :] = here * qs_ref[i * PARTS : i * PARTS + 1, :]
        rim_ref[modes + RIM + i : modes + RIM + i + 1, :] = here * long_ref[i * PARTS : i * PARTS + 1, :]


def back_local(mixed_ref, qs_ref, poles_ref, residues_ref, local_ref):
    tokens, width = qs_ref.shape
    modes = poles_ref.shape[0]
    steps = tokens // PARTS
    for block, lanes in lane_blocks(width):
        poles = [spread(row) for row in rows_of(poles_ref, lanes)]
        residues = [spread(row) for row in rows_of(residues_ref, lanes)]

        def step(back, states):
            i = steps - 1 - back
            rows = pl.ds(pl.multiple_of(i * PARTS, PARTS), PARTS)
            fresh = mixed_ref[rows, lanes] * qs_ref[rows, lanes]
            states = tuple(p * s + fresh for p, s in zip(poles, states))
            local_ref[rows, lanes] = mixed(residues, states)
            return states

        zero = jnp.zeros((PARTS, LANES), jnp.float32)
        lax.fori_loop(0, steps, step, (zero,) * modes, unroll=4)


def short_back(value, rim, taps_ref, which, target, natural):
    tokens, width = target.shape
    tap_count = taps_ref.shape[1]
    steps = tokens // PARTS
    bottom = lax.broadcasted_iota(jnp.int32, (PARTS, LANES), 0) == PARTS - 1
    for block, lanes in lane_blocks(width):
        taps = [spread(taps_ref[which, j : j + 1, lanes]) for j in range(tap_count)]

        def tap_step(back, window):
            i = steps - 1 - back
            window = (value(pl.ds(pl.multiple_of(i * PARTS, PARTS), PARTS), lanes),) + window
            total = taps[0] * window[0]
            for j in range(1, tap_count):
                total = total + taps[j] * window[j]
            natural[block, pl.ds(i, PARTS, stride=steps), :] = total
            return window[:-1]

        after = tuple(
            jnp.where(
                bottom,
                spread(rim(d, lanes)),
                pltpu.roll(value(pl.ds(d * PARTS, PARTS), lanes), PARTS - 1, 0),
            )
            for d in range(tap_count - 1)
        )
        lax.fori_loop(0, steps, tap_step, after, unroll=8)
    for block, lanes in lane_blocks(width):
        target[:, lanes] = natural[block].astype(target.dtype)


def back_query(mixed_ref, long_ref, next_ref, taps_ref, gq_ref, natural):
    first = next_ref.shape[0] - RIM
    short_back(
        lambda rows, lanes: mixed_ref[rows, lanes] * long_ref[rows, lanes],
        lambda d, lanes: next_ref[first + d : first + d + 1, lanes],
        taps_ref, 0, gq_ref, natural,
    )


def back_filters(local_ref, ks_ref, vs_ref, starts_ref, next_ref, beyond_ref, next_kv_ref, taps_ref, poles_ref, residues_ref, gk_ref, gv_ref, last, product, natural, rims):
    tokens, width = ks_ref.shape
    modes = poles_ref.shape[0]
    steps = tokens // PARTS
    poles_all = poles_ref[...]
    residues_all = residues_ref[...]
    entering = next_ref[0:modes, :] + power(poles_all, tokens - RIM) * beyond_ref[...]
    for i in range(RIM - 1, -1, -1):
        entering = poles_all * entering + next_ref[modes + i : modes + i + 1, :]
        here = jnp.sum(residues_all * entering, axis=0, keepdims=True)
        rims[0, i : i + 1, :] = here * next_kv_ref[1, i : i + 1, :]
        rims[1, i : i + 1, :] = here * next_kv_ref[0, i : i + 1, :]
    part_decay = power(poles_all, steps)
    for c in range(PARTS - 1, -1, -1):
        last[:, c, :] = residues_all * entering
        if c:
            entering = part_decay * entering + starts_ref[:, c, :]
    for block, lanes in lane_blocks(width):
        poles = [spread(row) for row in rows_of(poles_ref, lanes)]

        def step(back, fading):
            i = steps - 1 - back
            rows = pl.ds(pl.multiple_of(i * PARTS, PARTS), PARTS)
            fading = tuple(p * s for p, s in zip(poles, fading))
            product[rows, lanes] = local_ref[rows, lanes] + added(fading)
            return fading

        lax.fori_loop(0, steps, step, tuple(last[m, :, lanes] for m in range(modes)), unroll=4)
    for which, other, target in ((1, vs_ref, gk_ref), (2, ks_ref, gv_ref)):
        short_back(
            lambda rows, lanes: product[rows, lanes] * other[rows, lanes],
            lambda d, lanes: rims[which - 1, d : d + 1, lanes],
            taps_ref, which, target, natural,
        )


def pick_shares(place_ref, weight_ref, up_ref, down_ref, arrived):
    rows = weight_ref.shape[0] // 2
    blocks = arrived.shape[2]
    depth = up_ref.shape[1]
    width = depth // blocks
    count = weight_ref.shape[1] // depth
    first = pl.multiple_of(place_ref[2] * rows, rows)
    copies = []
    for side, (message_ref, step) in enumerate(((up_ref, 1), (down_ref, count - 1))):
        for part, (x, begin, size, target) in enumerate(
            (
                (lax.rem(place_ref[0] + step, count), 0, rows, 0),
                (lax.rem(place_ref[0] + 2, count), side * (rows // 2), rows // 2, rows),
            )
        ):
            for z in range(blocks):
                column = pl.multiple_of((z * count + x) * width, width)
                copies.append(
                    pltpu.make_async_copy(
                        weight_ref.at[pl.ds(first + begin, size), pl.ds(column, width)],
                        message_ref.at[pl.ds(target, size), pl.ds(z * width, width)],
                        arrived.at[side, part, z],
                    )
                )
    for copy in copies:
        copy.start()
    for copy in copies:
        copy.wait()


def join_shares(place_ref, share, other, weight):
    rows = share.shape[0]
    core = place_ref[2]
    weight[pl.ds(pl.multiple_of(core * rows, rows), rows), :] = share
    weight[pl.ds(pl.multiple_of((1 - core) * rows, rows), rows), :] = other


def ring_product(target_ref, ring, weight_ref, column_of, first=True):
    tokens, width = target_ref.shape
    rows = tokens // 2
    for n, refs in ring:
        for half in range(2):
            target_rows = pl.ds(half * rows, rows)
            features = refs[half][...] if len(refs) == 2 else refs[0][target_rows, :]
            term = lax.dot_general(
                features,
                weight_ref[:, pl.ds(column_of(n), width)],
                (((1,), (1,)), ((), ())),
                preferred_element_type=jnp.float32,
            )
            target_ref[target_rows, :] = term if first else target_ref[target_rows, :] + term
        first = False


def early_places(early_ref):
    count = early_ref.shape[0] + 3
    return [(n % count, (early_ref.at[n + 2],)) for n in range(-2, 3)]


def late_places(count, left_ref, right_ref, *middle):
    ring = [(3, (left_ref,)), (count - 3, (right_ref,))]
    return ring + [(count // 2, middle)] if middle else ring


def in_places(early_ref, *late_refs):
    return early_places(early_ref) + late_places(early_ref.shape[0] + 3, *late_refs)


def own_columns(place_ref, count, along_x, width):
    def column_of(n):
        block = lax.rem(place_ref[3] + n, count) * along_x + place_ref[0]
        return pl.multiple_of(block * width, width)

    return column_of


def keep_start(place_ref, weight_ref, *refs):
    *block_refs, early_ref, kept_ref, arrived = refs
    copies = [
        pltpu.make_async_copy(ref, early_ref.at[n], arrived.at[n]) for n, ref in enumerate(block_refs)
    ]
    for copy in copies:
        copy.start()
    for copy in copies:
        copy.wait()
    width = kept_ref.shape[1]
    count = early_ref.shape[0] + 3
    column_of = own_columns(place_ref, count, weight_ref.shape[1] // (count * width), width)
    ring_product(kept_ref, early_places(early_ref), weight_ref, column_of)


def keep_finish(place_ref, weight_ref, started_ref, *refs):
    *late_refs, kept_ref = refs
    width = kept_ref.shape[1]
    count = RING
    column_of = own_columns(place_ref, count, weight_ref.shape[1] // (count * width), width)
    kept_ref[...] = started_ref[...]
    ring_product(kept_ref, late_places(count, *late_refs), weight_ref, column_of, False)


def encode_tile(total, coded_ref, tile):
    largest = jnp.max(jnp.abs(total), axis=0, keepdims=True) * 1.01
    largest = jnp.maximum(largest, TINY).astype(jnp.bfloat16)
    scaled = total * (SPAN / largest.astype(jnp.float32))
    square = scaled * scaled
    fourth = square * square
    eighth = fourth * fourth
    code = jnp.where(scaled < 0, -eighth, eighth)
    start = pl.multiple_of(tile * (TILE + HEAD), HEAD)
    coded_ref[pl.ds(start, HEAD), :] = jnp.broadcast_to(largest, (HEAD, largest.shape[1]))
    coded_ref[pl.ds(start + HEAD, TILE), :] = code.astype(jnp.bfloat16)


def column_on_ring(place_ref, count, width):
    return lambda n: pl.multiple_of(lax.rem(place_ref[3] + n, count) * width, width)


def far_start(place_ref, *refs):
    *ring_refs, share_ref, other_ref, far_ref, weight = refs
    width = far_ref.shape[1]
    join_shares(place_ref, share_ref[...], other_ref[...], weight)
    column_of = column_on_ring(place_ref, weight.shape[1] // width, width)
    ring_product(far_ref, in_places(*ring_refs), weight, column_of)


def far_finish(place_ref, far_ref, middle_up_ref, middle_down_ref, share_ref, other_ref, up_ref, down_ref, weight):
    half, width = middle_up_ref.shape
    count = share_ref.shape[1] // width
    column = pl.ds(column_on_ring(place_ref, count, width)(count // 2), width)
    join_shares(place_ref, share_ref[:, column], other_ref[:, column], weight)
    for side, (features_ref, coded_ref) in enumerate(((middle_up_ref, up_ref), (middle_down_ref, down_ref))):
        for t in range(half // TILE):
            term = lax.dot_general(
                features_ref[t * TILE : (t + 1) * TILE, :],
                weight[...],
                (((1,), (1,)), ((), ())),
                preferred_element_type=jnp.float32,
            )
            row = side * half + t * TILE
            encode_tile(far_ref[row : row + TILE, :] + term, coded_ref, t)


def near_products(place_ref, *refs):
    *ring_refs, shares_ref, other_ref, next_ref, last_ref, weight = refs
    width = next_ref.shape[1]
    column_of = column_on_ring(place_ref, weight.shape[1] // width, width)
    for j, target in enumerate((next_ref, last_ref)):
        join_shares(place_ref, shares_ref[j], other_ref[j], weight)
        ring_product(target, in_places(*ring_refs), weight, column_of)


def send_half(next_ref, last_ref, next_coded_ref, last_coded_ref):
    tiles = next_ref.shape[0] // TILE
    half = tiles // 2
    for t in range(half):
        start = (half + t) * TILE
        encode_tile(next_ref[start : start + TILE, :], next_coded_ref, t)
        encode_tile(last_ref[t * TILE : (t + 1) * TILE, :], last_coded_ref, t)


def send_joined(next_ref, last_ref, up_ref, down_ref, next_coded_ref, last_coded_ref):
    tiles = next_ref.shape[0] // TILE
    half = tiles // 2
    everything = pl.ds(0, next_ref.shape[1])
    for t in range(half):
        coded = t * (TILE + HEAD)
        start = (half + t) * TILE
        after = next_ref[t * TILE : (t + 1) * TILE, :]
        before = last_ref[start : start + TILE, :]
        after = after + decoded(up_ref, coded, pl.ds(0, TILE), everything)
        before = before + decoded(down_ref, coded, pl.ds(0, TILE), everything)
        encode_tile(after, next_coded_ref, t)
        encode_tile(before, last_coded_ref, t)


def decoded(coded_ref, start, rows, lanes):
    largest = coded_ref[pl.ds(start, HEAD), lanes].astype(jnp.float32)[0:1]
    code = coded_ref[pl.ds(start + HEAD + rows.start, rows.size), lanes].astype(jnp.float32)
    size = jnp.exp2(jnp.log2(jnp.maximum(jnp.abs(code), LEAST)) * 0.125)
    value = jnp.where(code < 0, -size, size) * (largest * (1.0 / SPAN))
    return jnp.where(code == 0, 0.0, value)


def local_call(kernel, outs, scratch, operands, cost):
    whole = pl.BlockSpec(memory_space=pltpu.VMEM)
    return pl.pallas_call(
        kernel,
        out_shape=outs,
        in_specs=[whole if o.ndim > 1 else pl.BlockSpec(memory_space=pltpu.SMEM) for o in operands],
        out_specs=[whole] * len(outs),
        scratch_shapes=scratch,
        compiler_params=pltpu.CompilerParams(vmem_limit_bytes=VMEM_LIMIT),
        cost_estimate=pl.CostEstimate(flops=cost, bytes_accessed=cost // 64, transcendentals=0),
    )(*operands)


def floats(*shape):
    return jax.ShapeDtypeStruct(shape, jnp.float32)


def shift(block, axis, distance, size):
    return lax.ppermute(block, axis, [(i, (i + distance) % size) for i in range(size)])


def from_behind(block, axis, distance, size):
    return lax.ppermute(
        block, axis, [(i - distance, i) for i in range(size) if 0 <= i - distance < size]
    )


def shards(
    sizes, query_in, key_in, value_in, short_taps, modal_poles, modal_residues, out_weight, grad_out
):
    ctx_count, z_count, x_count = sizes
    tokens, width = query_in.shape
    modes = modal_poles.shape[0]
    slab = floats(tokens, width)
    rounded = jax.ShapeDtypeStruct((tokens, width), jnp.bfloat16)
    per_part = floats(modes, PARTS, width)
    state = floats(modes, width)
    slab_scratch = pltpu.VMEM((tokens, width), jnp.float32)
    natural_scratch = pltpu.VMEM((width // LANES, tokens, LANES), jnp.float32)
    part_scratch = pltpu.VMEM((modes, PARTS, width), jnp.float32)
    together = lax.optimization_barrier
    decay_1 = power(modal_poles, tokens)
    decay_2 = decay_1 * decay_1

    ctx = lax.axis_index("ctx")
    place = jnp.stack([lax.axis_index("x"), ctx // 2, ctx % 2, lax.axis_index("z")])

    right_1 = shift(grad_out, "z", 1, z_count)
    left_1 = shift(grad_out, "z", -1, z_count)
    tails = jnp.stack([a[tokens - 16 :] for a in (query_in, key_in, value_in)])
    prior = from_behind(tails, "ctx", 1, ctx_count)
    place, prior = together((place, prior))
    message = jax.ShapeDtypeStruct((width // 4 * 3, z_count * width), jnp.bfloat16)
    up, down = pl.pallas_call(
        pick_shares,
        out_shape=[message] * 2,
        in_specs=[pl.BlockSpec(memory_space=pltpu.SMEM), pl.BlockSpec(memory_space=pltpu.HBM)],
        out_specs=[pl.BlockSpec(memory_space=pltpu.VMEM)] * 2,
        scratch_shapes=[pltpu.SemaphoreType.DMA((2, 2, z_count))],
        compiler_params=pltpu.CompilerParams(vmem_limit_bytes=VMEM_LIMIT),
    )(place, out_weight)
    up = shift(up, "x", 1, x_count)
    down = shift(down, "x", -1, x_count)
    q_short, k_short, v_short, ends, own_end, first_kv = local_call(
        short_filters,
        [slab, slab, slab, per_part, state, floats(2, RIM, width)],
        [pltpu.VMEM((width // LANES, tokens + RIM, LANES), jnp.float32)],
        (query_in, key_in, value_in, prior, short_taps, modal_poles),
        tokens * width * 80,
    )
    right_2 = shift(right_1, "z", 1, z_count)
    left_2 = shift(left_1, "z", -1, z_count)
    one = from_behind(own_end, "ctx", 1, ctx_count)
    two = from_behind(own_end, "ctx", 2, ctx_count)
    seven = from_behind(own_end, "ctx", 7, ctx_count)
    triple = own_end + decay_1 * one + decay_2 * two
    right_2, left_2, triple, up, down = together((right_2, left_2, triple, up, down))

    right_3 = shift(right_2, "z", 1, z_count)
    left_3 = shift(left_2, "z", -1, z_count)
    rows = width // 2
    far_up = shift(up[rows:], "x", 1, x_count)
    far_down = shift(down[rows:], "x", -1, x_count)
    anywhere = pl.BlockSpec(memory_space=pl.ANY)
    in_vmem = pl.BlockSpec(memory_space=pltpu.VMEM)
    blocks = (right_2, right_1, grad_out, left_1, left_2)
    early, kept = pl.pallas_call(
        keep_start,
        out_shape=[jax.ShapeDtypeStruct((len(blocks), tokens, width), jnp.bfloat16), slab],
        in_specs=[pl.BlockSpec(memory_space=pltpu.SMEM), in_vmem] + [anywhere] * len(blocks),
        out_specs=[in_vmem] * 2,
        scratch_shapes=[pltpu.SemaphoreType.DMA((len(blocks),))],
        compiler_params=pltpu.CompilerParams(vmem_limit_bytes=VMEM_LIMIT),
        cost_estimate=pl.CostEstimate(
            flops=tokens * width * width * 10, bytes_accessed=tokens * width * 24, transcendentals=0
        ),
    )(place, out_weight, *blocks)
    near_shares, triple, kept = together((jnp.stack([down[:rows], up[:rows]]), triple, kept))
    other_near = lax.ppermute(near_shares, "ctx", [(i, i ^ 1) for i in range(ctx_count)])
    decay_3 = decay_2 * decay_1
    before = (
        from_behind(triple, "ctx", 1, ctx_count)
        + decay_3 * from_behind(triple, "ctx", 4, ctx_count)
        + decay_3 * decay_3 * seven
    )
    long_out, gated = local_call(
        long_forward,
        [slab, rounded],
        [part_scratch, natural_scratch],
        (q_short, k_short, v_short, ends, before, modal_poles, modal_residues),
        tokens * width * 70,
    )
    right_3, left_3, far_up, far_down, early, kept, gated, other_near = together(
        (right_3, left_3, far_up, far_down, early, kept, gated, other_near)
    )

    middle_up = shift(right_3[: tokens // 2], "z", 1, z_count)
    middle_down = shift(left_3[tokens // 2 :], "z", -1, z_count)
    far_share = jnp.concatenate([far_up, far_down])
    other_far = lax.ppermute(far_share, "ctx", [(i, i ^ 1) for i in range(ctx_count)])

    weight_scratch = pltpu.VMEM((width, z_count * width), jnp.bfloat16)
    product_cost = tokens * width * z_count * width * 2
    half_code = jax.ShapeDtypeStruct((tokens // TILE // 2 * (TILE + HEAD), width), jnp.bfloat16)
    (far,) = local_call(
        far_start,
        [slab],
        [weight_scratch],
        (place, early, left_3, right_3, far_share, other_far),
        product_cost,
    )
    middle_up, middle_down, far = together((middle_up, middle_down, far))
    on_ring = (early, left_3, right_3, middle_up, middle_down)
    up, down = local_call(
        far_finish,
        [half_code, half_code],
        [pltpu.VMEM((width, width), jnp.bfloat16)],
        (place, far, middle_up, middle_down, far_share, other_far),
        product_cost // z_count,
    )
    up = shift(up, "x", 1, x_count)
    down = shift(down, "x", -1, x_count)
    after, last = local_call(
        near_products,
        [slab, slab],
        [weight_scratch],
        (place, *on_ring, near_shares, other_near),
        2 * product_cost,
    )
    after_2, last_1 = local_call(
        send_half, [half_code, half_code], [], (after, last), tokens * width * 16
    )
    after_2 = shift(after_2, "x", 1, x_count)
    last_1 = shift(last_1, "x", -1, x_count)
    after_1, last_2 = local_call(
        send_joined, [half_code, half_code], [], (after, last, up, down), tokens * width * 32
    )
    after_1 = shift(after_1, "x", 1, x_count)
    last_2 = shift(last_2, "x", -1, x_count)
    (kept,) = local_call(
        keep_finish, [slab], [], (place, out_weight, kept, *on_ring[1:]), product_cost // 2
    )
    after_1, after_2, last_1, last_2, kept = together((after_1, after_2, last_1, last_2, kept))
    mixed_steps, starts, own_start, rim = local_call(
        back_states,
        [slab, per_part, state, floats(modes + 2 * RIM, width)],
        [part_scratch, natural_scratch],
        (kept, after_1, after_2, last_1, last_2, q_short, long_out, modal_poles),
        tokens * width * 40,
    )

    near = from_behind(jnp.concatenate([rim, own_start]), "ctx", -1, ctx_count)
    (local,) = local_call(
        back_local, [slab], [], (mixed_steps, q_short, modal_poles, modal_residues), tokens * width * 64
    )
    two = from_behind(own_start, "ctx", -2, ctx_count)
    next_kv = from_behind(first_kv, "ctx", -1, ctx_count)
    near, two, local, next_kv = together((near, two, local, next_kv))
    rim_size = modes + 2 * RIM
    near_rim = near[:rim_size]
    triple = own_start + decay_1 * near[rim_size:] + decay_2 * two
    triple_2 = from_behind(triple, "ctx", -2, ctx_count)
    triple_5 = from_behind(triple, "ctx", -5, ctx_count)
    (grad_query,) = local_call(
        back_query,
        [rounded],
        [natural_scratch],
        (mixed_steps, long_out, near_rim, short_taps),
        tokens * width * 20,
    )
    triple_2, triple_5, grad_query = together((triple_2, triple_5, grad_query))
    beyond = triple_2 + decay_2 * decay_1 * triple_5
    grad_key, grad_value = local_call(
        back_filters,
        [rounded, rounded],
        [part_scratch, slab_scratch, natural_scratch, pltpu.VMEM((2, RIM, width), jnp.float32)],
        (
            local, k_short, v_short, starts, near_rim, beyond, next_kv,
            short_taps, modal_poles, modal_residues,
        ),
        tokens * width * 80,
    )
    return gated, grad_query, grad_key, grad_value


def solution(mesh):
    ctx_count, tp_count = mesh.shape["ctx"], mesh.shape["tp"]
    sizes = (ctx_count, tp_count // X_COUNT, X_COUNT)
    grid = Mesh(mesh.devices.reshape(sizes), ("ctx", "z", "x"))
    tp = ("z", "x")
    placed = (
        P("ctx", tp),
        P("ctx", tp),
        P("ctx", tp),
        P(None, None, tp),
        P(None, tp),
        P(None, tp),
        P(tp, None),
        P("ctx", tp),
    )
    return jax.shard_map(
        functools.partial(shards, sizes),
        mesh=grid,
        in_specs=placed,
        out_specs=(P("ctx", tp),) * 4,
        check_vma=False,
    )
```

```python
import functools
import jax
import jax.numpy as jnp
from jax import lax
from jax.experimental import pallas as pl
from jax.experimental.pallas import tpu as pltpu
from jax.sharding import Mesh, PartitionSpec as P

LANES = 128
PARTS = 8
RIM = 8
X_COUNT = 4
RING = 8
TILE = 256
HEAD = 16
SPAN = 32768.0
TINY = 1e-30
LEAST = 1e-37
VMEM_LIMIT = 16 * 1024 * 1024


def power(base, exponent):
    result = None
    while exponent:
        if exponent & 1:
            result = base if result is None else result * base
        exponent >>= 1
        if exponent:
            base = base * base
    return result


def rows_of(ref, lanes):
    return [ref[m : m + 1, lanes] for m in range(ref.shape[0])]


def spread(row):
    return jnp.broadcast_to(row, (PARTS, LANES))


def lane_blocks(width):
    return [(n, pl.ds(n * LANES, LANES)) for n in range(width // LANES)]


def short_filters(q_ref, k_ref, v_ref, prior_ref, taps_ref, poles_ref, qs_ref, ks_ref, vs_ref, ends_ref, own_ref, first_ref, natural):
    tokens, width = q_ref.shape
    tap_count = taps_ref.shape[1]
    modes = poles_ref.shape[0]
    steps = tokens // PARTS
    for which, (source, target) in enumerate(((q_ref, qs_ref), (k_ref, ks_ref), (v_ref, vs_ref))):
        for block, lanes in lane_blocks(width):
            natural[block, 0:RIM, :] = prior_ref[which, :, lanes].astype(jnp.float32)[prior_ref.shape[1] - RIM :]
            natural[block, RIM:, :] = source[:, lanes].astype(jnp.float32)
        for block, lanes in lane_blocks(width):
            taps = [spread(taps_ref[which, j : j + 1, lanes]) for j in range(tap_count)]

            def tap_step(i, window):
                fresh = natural[block, pl.ds(RIM + i, PARTS, stride=steps), :]
                window = (fresh,) + window
                total = taps[0] * window[0]
                for j in range(1, tap_count):
                    total = total + taps[j] * window[j]
                target[pl.ds(pl.multiple_of(i * PARTS, PARTS), PARTS), lanes] = total
                return window[:-1]

            before = tuple(
                natural[block, pl.ds(RIM - 1 - d, PARTS, stride=steps), :] for d in range(tap_count - 1)
            )
            lax.fori_loop(0, steps, tap_step, before, unroll=8)
    for block, lanes in lane_blocks(width):
        poles = [spread(row) for row in rows_of(poles_ref, lanes)]

        def state_step(i, states):
            rows = pl.ds(pl.multiple_of(i * PARTS, PARTS), PARTS)
            fresh = ks_ref[rows, lanes] * vs_ref[rows, lanes]
            return tuple(p * s + fresh for p, s in zip(poles, states))

        zero = jnp.zeros((PARTS, LANES), jnp.float32)
        states = lax.fori_loop(0, steps, state_step, (zero,) * modes, unroll=4)
        for m in range(modes):
            ends_ref[m, :, lanes] = states[m]
    part_decay = power(poles_ref[...], steps)
    own = ends_ref[:, 0, :]
    for c in range(1, PARTS):
        own = part_decay * own + ends_ref[:, c, :]
    own_ref[...] = own
    for i in range(RIM):
        first_ref[0, i : i + 1, :] = ks_ref[i * PARTS : i * PARTS + 1, :]
        first_ref[1, i : i + 1, :] = vs_ref[i * PARTS : i * PARTS + 1, :]


def long_forward(qs_ref, ks_ref, vs_ref, ends_ref, before_ref, poles_ref, residues_ref, long_ref, gated_ref, first, natural):
    tokens, width = qs_ref.shape
    modes = poles_ref.shape[0]
    steps = tokens // PARTS
    part_decay = power(poles_ref[...], steps)
    entering = before_ref[...]
    for c in range(PARTS):
        first[:, c, :] = entering
        if c < PARTS - 1:
            entering = part_decay * entering + ends_ref[:, c, :]
    for block, lanes in lane_blocks(width):
        poles = [spread(row) for row in rows_of(poles_ref, lanes)]
        residues = [spread(row) for row in rows_of(residues_ref, lanes)]

        def step(i, states):
            rows = pl.ds(pl.multiple_of(i * PARTS, PARTS), PARTS)
            fresh = ks_ref[rows, lanes] * vs_ref[rows, lanes]
            states = tuple(p * s + fresh for p, s in zip(poles, states))
            total = mixed(residues, states)
            long_ref[rows, lanes] = total
            natural[block, pl.ds(i, PARTS, stride=steps), :] = total * qs_ref[rows, lanes]
            return states

        lax.fori_loop(0, steps, step, tuple(first[m, :, lanes] for m in range(modes)), unroll=4)
    for block, lanes in lane_blocks(width):
        gated_ref[:, lanes] = natural[block].astype(gated_ref.dtype)


def mixed(residues, states):
    return added([r * s for r, s in zip(residues, states)])


def added(terms):
    while len(terms) > 1:
        terms = [a + b for a, b in zip(terms[::2], terms[1::2])] + list(terms[len(terms) // 2 * 2 :])
    return terms[0]


def back_states(kept_ref, one_up_ref, one_down_ref, three_up_ref, three_down_ref, qs_ref, long_ref, poles_ref, mixed_ref, starts_ref, own_ref, rim_ref, rim_starts, natural):
    tokens, width = qs_ref.shape
    modes = poles_ref.shape[0]
    steps = tokens // PARTS
    for block, lanes in lane_blocks(width):
        poles = [spread(row) for row in rows_of(poles_ref, lanes)]

        for half, refs in enumerate(((one_up_ref, three_up_ref), (one_down_ref, three_down_ref))):

            def add_step(n, carry):
                piece = 64
                row = pl.multiple_of(n * piece, piece)
                tile, inside = row // TILE, pl.multiple_of(row % TILE, piece)
                there = pl.ds(pl.multiple_of(half * (tokens // 2) + row, piece), piece)
                total = kept_ref[there, lanes]
                for ref in refs:
                    start = pl.multiple_of(tile * (TILE + HEAD), HEAD)
                    total = total + decoded(ref, start, pl.ds(inside, piece), lanes)
                natural[block, there, :] = total
                return carry

            lax.fori_loop(0, tokens // 128, add_step, 0)

        def step(back, states):
            i = steps - 1 - back
            rows = pl.ds(pl.multiple_of(i * PARTS, PARTS), PARTS)
            here = natural[block, pl.ds(i, PARTS, stride=steps), :]
            mixed_ref[rows, lanes] = here
            fresh = here * qs_ref[rows, lanes]
            return tuple(p * s + fresh for p, s in zip(poles, states))

        zero = jnp.zeros((PARTS, LANES), jnp.float32)
        states = lax.fori_loop(0, steps - RIM, step, (zero,) * modes, unroll=4)
        for m in range(modes):
            rim_starts[m, :, lanes] = states[m]
        states = lax.fori_loop(steps - RIM, steps, step, states, unroll=4)
        for m in range(modes):
            starts_ref[m, :, lanes] = states[m]
    part_decay = power(poles_ref[...], steps)
    own = starts_ref[:, PARTS - 1, :]
    for c in range(PARTS - 2, 0, -1):
        own = part_decay * own + starts_ref[:, c, :]
    own_ref[...] = part_decay * own + starts_ref[:, 0, :]
    rim_ref[0:modes, :] = power(poles_ref[...], steps - RIM) * own + rim_starts[:, 0, :]
    for i in range(RIM):
        here = mixed_ref[i * PARTS : i * PARTS + 1, :]
        rim_ref[modes + i : modes + i + 1, :] = here * qs_ref[i * PARTS : i * PARTS + 1, :]
        rim_ref[modes + RIM + i : modes + RIM + i + 1, :] = here * long_ref[i * PARTS : i * PARTS + 1, :]


def back_local(mixed_ref, qs_ref, poles_ref, residues_ref, local_ref):
    tokens, width = qs_ref.shape
    modes = poles_ref.shape[0]
    steps = tokens // PARTS
    for block, lanes in lane_blocks(width):
        poles = [spread(row) for row in rows_of(poles_ref, lanes)]
        residues = [spread(row) for row in rows_of(residues_ref, lanes)]

        def step(back, states):
            i = steps - 1 - back
            rows = pl.ds(pl.multiple_of(i * PARTS, PARTS), PARTS)
            fresh = mixed_ref[rows, lanes] * qs_ref[rows, lanes]
            states = tuple(p * s + fresh for p, s in zip(poles, states))
            local_ref[rows, lanes] = mixed(residues, states)
            return states

        zero = jnp.zeros((PARTS, LANES), jnp.float32)
        lax.fori_loop(0, steps, step, (zero,) * modes, unroll=4)


def short_back(value, rim, taps_ref, which, target, natural):
    tokens, width = target.shape
    tap_count = taps_ref.shape[1]
    steps = tokens // PARTS
    bottom = lax.broadcasted_iota(jnp.int32, (PARTS, LANES), 0) == PARTS - 1
    for block, lanes in lane_blocks(width):
        taps = [spread(taps_ref[which, j : j + 1, lanes]) for j in range(tap_count)]

        def tap_step(back, window):
            i = steps - 1 - back
            window = (value(pl.ds(pl.multiple_of(i * PARTS, PARTS), PARTS), lanes),) + window
            total = taps[0] * window[0]
            for j in range(1, tap_count):
                total = total + taps[j] * window[j]
            natural[block, pl.ds(i, PARTS, stride=steps), :] = total
            return window[:-1]

        after = tuple(
            jnp.where(
                bottom,
                spread(rim(d, lanes)),
                pltpu.roll(value(pl.ds(d * PARTS, PARTS), lanes), PARTS - 1, 0),
            )
            for d in range(tap_count - 1)
        )
        lax.fori_loop(0, steps, tap_step, after, unroll=8)
    for block, lanes in lane_blocks(width):
        target[:, lanes] = natural[block].astype(target.dtype)


def back_query(mixed_ref, long_ref, next_ref, taps_ref, gq_ref, natural):
    first = next_ref.shape[0] - RIM
    short_back(
        lambda rows, lanes: mixed_ref[rows, lanes] * long_ref[rows, lanes],
        lambda d, lanes: next_ref[first + d : first + d + 1, lanes],
        taps_ref, 0, gq_ref, natural,
    )


def back_filters(local_ref, ks_ref, vs_ref, starts_ref, next_ref, beyond_ref, next_kv_ref, taps_ref, poles_ref, residues_ref, gk_ref, gv_ref, last, product, natural, rims):
    tokens, width = ks_ref.shape
    modes = poles_ref.shape[0]
    steps = tokens // PARTS
    poles_all = poles_ref[...]
    residues_all = residues_ref[...]
    entering = next_ref[0:modes, :] + power(poles_all, tokens - RIM) * beyond_ref[...]
    for i in range(RIM - 1, -1, -1):
        entering = poles_all * entering + next_ref[modes + i : modes + i + 1, :]
        here = jnp.sum(residues_all * entering, axis=0, keepdims=True)
        rims[0, i : i + 1, :] = here * next_kv_ref[1, i : i + 1, :]
        rims[1, i : i + 1, :] = here * next_kv_ref[0, i : i + 1, :]
    part_decay = power(poles_all, steps)
    for c in range(PARTS - 1, -1, -1):
        last[:, c, :] = residues_all * entering
        if c:
            entering = part_decay * entering + starts_ref[:, c, :]
    for block, lanes in lane_blocks(width):
        poles = [spread(row) for row in rows_of(poles_ref, lanes)]

        def step(back, fading):
            i = steps - 1 - back
            rows = pl.ds(pl.multiple_of(i * PARTS, PARTS), PARTS)
            fading = tuple(p * s for p, s in zip(poles, fading))
            product[rows, lanes] = local_ref[rows, lanes] + added(fading)
            return fading

        lax.fori_loop(0, steps, step, tuple(last[m, :, lanes] for m in range(modes)), unroll=4)
    for which, other, target in ((1, vs_ref, gk_ref), (2, ks_ref, gv_ref)):
        short_back(
            lambda rows, lanes: product[rows, lanes] * other[rows, lanes],
            lambda d, lanes: rims[which - 1, d : d + 1, lanes],
            taps_ref, which, target, natural,
        )


def pick_shares(place_ref, weight_ref, up_ref, down_ref, arrived):
    rows = weight_ref.shape[0] // 2
    blocks = arrived.shape[2]
    depth = up_ref.shape[1]
    width = depth // blocks
    count = weight_ref.shape[1] // depth
    first = pl.multiple_of(place_ref[2] * rows, rows)
    copies = []
    for side, (message_ref, step) in enumerate(((up_ref, 1), (down_ref, count - 1))):
        for part, (x, begin, size, target) in enumerate(
            (
                (lax.rem(place_ref[0] + step, count), 0, rows, 0),
                (lax.rem(place_ref[0] + 2, count), side * (rows // 2), rows // 2, rows),
            )
        ):
            for z in range(blocks):
                column = pl.multiple_of((z * count + x) * width, width)
                copies.append(
                    pltpu.make_async_copy(
                        weight_ref.at[pl.ds(first + begin, size), pl.ds(column, width)],
                        message_ref.at[pl.ds(target, size), pl.ds(z * width, width)],
                        arrived.at[side, part, z],
                    )
                )
    for copy in copies:
        copy.start()
    for copy in copies:
        copy.wait()


def join_shares(place_ref, share, other, weight):
    rows = share.shape[0]
    core = place_ref[2]
    weight[pl.ds(pl.multiple_of(core * rows, rows), rows), :] = share
    weight[pl.ds(pl.multiple_of((1 - core) * rows, rows), rows), :] = other


def ring_product(target_ref, ring, weight_ref, column_of, first=True):
    tokens, width = target_ref.shape
    rows = tokens // 2
    for n, refs in ring:
        for half in range(2):
            target_rows = pl.ds(half * rows, rows)
            features = refs[half][...] if len(refs) == 2 else refs[0][target_rows, :]
            term = lax.dot_general(
                features,
                weight_ref[:, pl.ds(column_of(n), width)],
                (((1,), (1,)), ((), ())),
                preferred_element_type=jnp.float32,
            )
            target_ref[target_rows, :] = term if first else target_ref[target_rows, :] + term
        first = False


def early_places(early_ref):
    count = early_ref.shape[0] + 3
    return [(n % count, (early_ref.at[n + 2],)) for n in range(-2, 3)]


def late_places(count, left_ref, right_ref, *middle):
    ring = [(3, (left_ref,)), (count - 3, (right_ref,))]
    return ring + [(count // 2, middle)] if middle else ring


def in_places(early_ref, *late_refs):
    return early_places(early_ref) + late_places(early_ref.shape[0] + 3, *late_refs)


def own_columns(place_ref, count, along_x, width):
    def column_of(n):
        block = lax.rem(place_ref[3] + n, count) * along_x + place_ref[0]
        return pl.multiple_of(block * width, width)

    return column_of


def keep_start(place_ref, weight_ref, *refs):
    *block_refs, early_ref, kept_ref, arrived = refs
    copies = [
        pltpu.make_async_copy(ref, early_ref.at[n], arrived.at[n]) for n, ref in enumerate(block_refs)
    ]
    for copy in copies:
        copy.start()
    for copy in copies:
        copy.wait()
    width = kept_ref.shape[1]
    count = early_ref.shape[0] + 3
    column_of = own_columns(place_ref, count, weight_ref.shape[1] // (count * width), width)
    ring_product(kept_ref, early_places(early_ref), weight_ref, column_of)


def keep_finish(place_ref, weight_ref, started_ref, *refs):
    *late_refs, kept_ref = refs
    width = kept_ref.shape[1]
    count = RING
    column_of = own_columns(place_ref, count, weight_ref.shape[1] // (count * width), width)
    kept_ref[...] = started_ref[...]
    ring_product(kept_ref, late_places(count, *late_refs), weight_ref, column_of, False)


def encode_tile(total, coded_ref, tile):
    largest = jnp.max(jnp.abs(total), axis=0, keepdims=True) * 1.01
    largest = jnp.maximum(largest, TINY).astype(jnp.bfloat16)
    scaled = total * (SPAN / largest.astype(jnp.float32))
    square = scaled * scaled
    fourth = square * square
    eighth = fourth * fourth
    code = jnp.where(scaled < 0, -eighth, eighth)
    start = pl.multiple_of(tile * (TILE + HEAD), HEAD)
    coded_ref[pl.ds(start, HEAD), :] = jnp.broadcast_to(largest, (HEAD, largest.shape[1]))
    coded_ref[pl.ds(start + HEAD, TILE), :] = code.astype(jnp.bfloat16)


def column_on_ring(place_ref, count, width):
    return lambda n: pl.multiple_of(lax.rem(place_ref[3] + n, count) * width, width)


def far_start(place_ref, *refs):
    *ring_refs, share_ref, other_ref, far_ref, weight = refs
    width = far_ref.shape[1]
    join_shares(place_ref, share_ref[...], other_ref[...], weight)
    column_of = column_on_ring(place_ref, weight.shape[1] // width, width)
    ring_product(far_ref, in_places(*ring_refs), weight, column_of)


def far_finish(place_ref, far_ref, middle_up_ref, middle_down_ref, share_ref, other_ref, up_ref, down_ref, weight):
    half, width = middle_up_ref.shape
    count = share_ref.shape[1] // width
    column = pl.ds(column_on_ring(place_ref, count, width)(count // 2), width)
    join_shares(place_ref, share_ref[:, column], other_ref[:, column], weight)
    for side, (features_ref, coded_ref) in enumerate(((middle_up_ref, up_ref), (middle_down_ref, down_ref))):
        for t in range(half // TILE):
            term = lax.dot_general(
                features_ref[t * TILE : (t + 1) * TILE, :],
                weight[...],
                (((1,), (1,)), ((), ())),
                preferred_element_type=jnp.float32,
            )
            row = side * half + t * TILE
            encode_tile(far_ref[row : row + TILE, :] + term, coded_ref, t)


def near_products(place_ref, *refs):
    *ring_refs, shares_ref, other_ref, next_ref, last_ref, weight = refs
    width = next_ref.shape[1]
    column_of = column_on_ring(place_ref, weight.shape[1] // width, width)
    for j, target in enumerate((next_ref, last_ref)):
        join_shares(place_ref, shares_ref[j], other_ref[j], weight)
        ring_product(target, in_places(*ring_refs), weight, column_of)


def send_half(next_ref, last_ref, next_coded_ref, last_coded_ref):
    tiles = next_ref.shape[0] // TILE
    half = tiles // 2
    for t in range(half):
        start = (half + t) * TILE
        encode_tile(next_ref[start : start + TILE, :], next_coded_ref, t)
        encode_tile(last_ref[t * TILE : (t + 1) * TILE, :], last_coded_ref, t)


def send_joined(next_ref, last_ref, up_ref, down_ref, next_coded_ref, last_coded_ref):
    tiles = next_ref.shape[0] // TILE
    half = tiles // 2
    everything = pl.ds(0, next_ref.shape[1])
    for t in range(half):
        coded = t * (TILE + HEAD)
        start = (half + t) * TILE
        after = next_ref[t * TILE : (t + 1) * TILE, :]
        before = last_ref[start : start + TILE, :]
        after = after + decoded(up_ref, coded, pl.ds(0, TILE), everything)
        before = before + decoded(down_ref, coded, pl.ds(0, TILE), everything)
        encode_tile(after, next_coded_ref, t)
        encode_tile(before, last_coded_ref, t)


def decoded(coded_ref, start, rows, lanes):
    largest = coded_ref[pl.ds(start, HEAD), lanes].astype(jnp.float32)[0:1]
    code = coded_ref[pl.ds(start + HEAD + rows.start, rows.size), lanes].astype(jnp.float32)
    size = jnp.exp2(jnp.log2(jnp.maximum(jnp.abs(code), LEAST)) * 0.125)
    value = jnp.where(code < 0, -size, size) * (largest * (1.0 / SPAN))
    return jnp.where(code == 0, 0.0, value)


def local_call(kernel, outs, scratch, operands, cost):
    whole = pl.BlockSpec(memory_space=pltpu.VMEM)
    return pl.pallas_call(
        kernel,
        out_shape=outs,
        in_specs=[whole if o.ndim > 1 else pl.BlockSpec(memory_space=pltpu.SMEM) for o in operands],
        out_specs=[whole] * len(outs),
        scratch_shapes=scratch,
        compiler_params=pltpu.CompilerParams(vmem_limit_bytes=VMEM_LIMIT),
        cost_estimate=pl.CostEstimate(flops=cost, bytes_accessed=cost // 64, transcendentals=0),
    )(*operands)


def floats(*shape):
    return jax.ShapeDtypeStruct(shape, jnp.float32)


def shift(block, axis, distance, size):
    return lax.ppermute(block, axis, [(i, (i + distance) % size) for i in range(size)])


def from_behind(block, axis, distance, size):
    return lax.ppermute(
        block, axis, [(i - distance, i) for i in range(size) if 0 <= i - distance < size]
    )


def shards(
    sizes, query_in, key_in, value_in, short_taps, modal_poles, modal_residues, out_weight, grad_out
):
    ctx_count, z_count, x_count = sizes
    tokens, width = query_in.shape
    modes = modal_poles.shape[0]
    slab = floats(tokens, width)
    rounded = jax.ShapeDtypeStruct((tokens, width), jnp.bfloat16)
    per_part = floats(modes, PARTS, width)
    state = floats(modes, width)
    slab_scratch = pltpu.VMEM((tokens, width), jnp.float32)
    natural_scratch = pltpu.VMEM((width // LANES, tokens, LANES), jnp.float32)
    part_scratch = pltpu.VMEM((modes, PARTS, width), jnp.float32)
    together = lax.optimization_barrier
    decay_1 = power(modal_poles, tokens)
    decay_2 = decay_1 * decay_1

    ctx = lax.axis_index("ctx")
    place = jnp.stack([lax.axis_index("x"), ctx // 2, ctx % 2, lax.axis_index("z")])

    right_1 = shift(grad_out, "z", 1, z_count)
    left_1 = shift(grad_out, "z", -1, z_count)
    tails = jnp.stack([a[tokens - 16 :] for a in (query_in, key_in, value_in)])
    prior = from_behind(tails, "ctx", 1, ctx_count)
    place, prior = together((place, prior))
    message = jax.ShapeDtypeStruct((width // 4 * 3, z_count * width), jnp.bfloat16)
    up, down = pl.pallas_call(
        pick_shares,
        out_shape=[message] * 2,
        in_specs=[pl.BlockSpec(memory_space=pltpu.SMEM), pl.BlockSpec(memory_space=pltpu.HBM)],
        out_specs=[pl.BlockSpec(memory_space=pltpu.VMEM)] * 2,
        scratch_shapes=[pltpu.SemaphoreType.DMA((2, 2, z_count))],
        compiler_params=pltpu.CompilerParams(vmem_limit_bytes=VMEM_LIMIT),
    )(place, out_weight)
    up = shift(up, "x", 1, x_count)
    down = shift(down, "x", -1, x_count)
    q_short, k_short, v_short, ends, own_end, first_kv = local_call(
        short_filters,
        [slab, slab, slab, per_part, state, floats(2, RIM, width)],
        [pltpu.VMEM((width // LANES, tokens + RIM, LANES), jnp.float32)],
        (query_in, key_in, value_in, prior, short_taps, modal_poles),
        tokens * width * 80,
    )
    right_2 = shift(right_1, "z", 1, z_count)
    left_2 = shift(left_1, "z", -1, z_count)
    one = from_behind(own_end, "ctx", 1, ctx_count)
    pair = own_end + decay_1 * one
    two = from_behind(pair, "ctx", 2, ctx_count)
    right_2, left_2, two, up, down = together((right_2, left_2, two, up, down))

    right_3 = shift(right_2, "z", 1, z_count)
    left_3 = shift(left_2, "z", -1, z_count)
    rows = width // 2
    far_up = shift(up[rows:], "x", 1, x_count)
    far_down = shift(down[rows:], "x", -1, x_count)
    near_shares = jnp.stack([down[:rows], up[:rows]])
    other_near = lax.ppermute(near_shares, "ctx", [(i, i ^ 1) for i in range(ctx_count)])
    four = from_behind(pair + decay_2 * two, "ctx", 4, ctx_count)
    before = one + decay_1 * two + decay_2 * decay_1 * four
    long_out, gated = local_call(
        long_forward,
        [slab, rounded],
        [part_scratch, natural_scratch],
        (q_short, k_short, v_short, ends, before, modal_poles, modal_residues),
        tokens * width * 70,
    )
    anywhere = pl.BlockSpec(memory_space=pl.ANY)
    in_vmem = pl.BlockSpec(memory_space=pltpu.VMEM)
    blocks = (right_2, right_1, grad_out, left_1, left_2)
    early, kept = pl.pallas_call(
        keep_start,
        out_shape=[jax.ShapeDtypeStruct((len(blocks), tokens, width), jnp.bfloat16), slab],
        in_specs=[pl.BlockSpec(memory_space=pltpu.SMEM), in_vmem] + [anywhere] * len(blocks),
        out_specs=[in_vmem] * 2,
        scratch_shapes=[pltpu.SemaphoreType.DMA((len(blocks),))],
        compiler_params=pltpu.CompilerParams(vmem_limit_bytes=VMEM_LIMIT),
        cost_estimate=pl.CostEstimate(
            flops=tokens * width * width * 10, bytes_accessed=tokens * width * 24, transcendentals=0
        ),
    )(place, out_weight, *blocks)
    right_3, left_3, far_up, far_down, early, kept, gated, other_near = together(
        (right_3, left_3, far_up, far_down, early, kept, gated, other_near)
    )

    middle_up = shift(right_3[: tokens // 2], "z", 1, z_count)
    middle_down = shift(left_3[tokens // 2 :], "z", -1, z_count)
    far_share = jnp.concatenate([far_up, far_down])
    other_far = lax.ppermute(far_share, "ctx", [(i, i ^ 1) for i in range(ctx_count)])

    weight_scratch = pltpu.VMEM((width, z_count * width), jnp.bfloat16)
    product_cost = tokens * width * z_count * width * 2
    half_code = jax.ShapeDtypeStruct((tokens // TILE // 2 * (TILE + HEAD), width), jnp.bfloat16)
    (far,) = local_call(
        far_start,
        [slab],
        [weight_scratch],
        (place, early, left_3, right_3, far_share, other_far),
        product_cost,
    )
    middle_up, middle_down, far = together((middle_up, middle_down, far))
    on_ring = (early, left_3, right_3, middle_up, middle_down)
    up, down = local_call(
        far_finish,
        [half_code, half_code],
        [pltpu.VMEM((width, width), jnp.bfloat16)],
        (place, far, middle_up, middle_down, far_share, other_far),
        product_cost // z_count,
    )
    up = shift(up, "x", 1, x_count)
    down = shift(down, "x", -1, x_count)
    after, last = local_call(
        near_products,
        [slab, slab],
        [weight_scratch],
        (place, *on_ring, near_shares, other_near),
        2 * product_cost,
    )
    after_2, last_1 = local_call(
        send_half, [half_code, half_code], [], (after, last), tokens * width * 16
    )
    after_2 = shift(after_2, "x", 1, x_count)
    last_1 = shift(last_1, "x", -1, x_count)
    after_1, last_2 = local_call(
        send_joined, [half_code, half_code], [], (after, last, up, down), tokens * width * 32
    )
    after_1 = shift(after_1, "x", 1, x_count)
    last_2 = shift(last_2, "x", -1, x_count)
    (kept,) = local_call(
        keep_finish, [slab], [], (place, out_weight, kept, *on_ring[1:]), product_cost // 2
    )
    after_1, after_2, last_1, last_2, kept = together((after_1, after_2, last_1, last_2, kept))
    mixed_steps, starts, own_start, rim = local_call(
        back_states,
        [slab, per_part, state, floats(modes + 2 * RIM, width)],
        [part_scratch, natural_scratch],
        (kept, after_1, after_2, last_1, last_2, q_short, long_out, modal_poles),
        tokens * width * 40,
    )

    near = from_behind(jnp.concatenate([rim, own_start]), "ctx", -1, ctx_count)
    (local,) = local_call(
        back_local, [slab], [], (mixed_steps, q_short, modal_poles, modal_residues), tokens * width * 64
    )
    two = from_behind(own_start, "ctx", -2, ctx_count)
    next_kv = from_behind(first_kv, "ctx", -1, ctx_count)
    near, two, local, next_kv = together((near, two, local, next_kv))
    rim_size = modes + 2 * RIM
    near_rim = near[:rim_size]
    triple = own_start + decay_1 * near[rim_size:] + decay_2 * two
    triple_2 = from_behind(triple, "ctx", -2, ctx_count)
    triple_5 = from_behind(triple, "ctx", -5, ctx_count)
    (grad_query,) = local_call(
        back_query,
        [rounded],
        [natural_scratch],
        (mixed_steps, long_out, near_rim, short_taps),
        tokens * width * 20,
    )
    triple_2, triple_5, grad_query = together((triple_2, triple_5, grad_query))
    beyond = triple_2 + decay_2 * decay_1 * triple_5
    grad_key, grad_value = local_call(
        back_filters,
        [rounded, rounded],
        [part_scratch, slab_scratch, natural_scratch, pltpu.VMEM((2, RIM, width), jnp.float32)],
        (
            local, k_short, v_short, starts, near_rim, beyond, next_kv,
            short_taps, modal_poles, modal_residues,
        ),
        tokens * width * 80,
    )
    return gated, grad_query, grad_key, grad_value


def solution(mesh):
    ctx_count, tp_count = mesh.shape["ctx"], mesh.shape["tp"]
    sizes = (ctx_count, tp_count // X_COUNT, X_COUNT)
    grid = Mesh(mesh.devices.reshape(sizes), ("ctx", "z", "x"))
    tp = ("z", "x")
    placed = (
        P("ctx", tp),
        P("ctx", tp),
        P("ctx", tp),
        P(None, None, tp),
        P(None, tp),
        P(None, tp),
        P(tp, None),
        P("ctx", tp),
    )
    return jax.shard_map(
        functools.partial(shards, sizes),
        mesh=grid,
        in_specs=placed,
        out_specs=(P("ctx", tp),) * 4,
        check_vma=False,
    )
```

```python
import functools
import jax
import jax.numpy as jnp
from jax import lax
from jax.experimental import pallas as pl
from jax.experimental.pallas import tpu as pltpu
from jax.sharding import Mesh, PartitionSpec as P

LANES = 128
PARTS = 8
RIM = 8
X_COUNT = 4
RING = 8
TILE = 256
HEAD = 16
SPAN = 32768.0
TINY = 1e-30
LEAST = 1e-37
VMEM_LIMIT = 16 * 1024 * 1024


def power(base, exponent):
    result = None
    while exponent:
        if exponent & 1:
            result = base if result is None else result * base
        exponent >>= 1
        if exponent:
            base = base * base
    return result


def rows_of(ref, lanes):
    return [ref[m : m + 1, lanes] for m in range(ref.shape[0])]


def spread(row):
    return jnp.broadcast_to(row, (PARTS, LANES))


def lane_blocks(width):
    return [(n, pl.ds(n * LANES, LANES)) for n in range(width // LANES)]


def short_filters(q_ref, k_ref, v_ref, prior_ref, taps_ref, poles_ref, qs_ref, ks_ref, vs_ref, ends_ref, own_ref, first_ref, natural):
    tokens, width = q_ref.shape
    tap_count = taps_ref.shape[1]
    modes = poles_ref.shape[0]
    steps = tokens // PARTS
    for which, (source, target) in enumerate(((q_ref, qs_ref), (k_ref, ks_ref), (v_ref, vs_ref))):
        for block, lanes in lane_blocks(width):
            natural[block, 0:RIM, :] = prior_ref[which, :, lanes].astype(jnp.float32)[prior_ref.shape[1] - RIM :]
            natural[block, RIM:, :] = source[:, lanes].astype(jnp.float32)
        for block, lanes in lane_blocks(width):
            taps = [spread(taps_ref[which, j : j + 1, lanes]) for j in range(tap_count)]

            def tap_step(i, window):
                fresh = natural[block, pl.ds(RIM + i, PARTS, stride=steps), :]
                window = (fresh,) + window
                total = taps[0] * window[0]
                for j in range(1, tap_count):
                    total = total + taps[j] * window[j]
                target[pl.ds(pl.multiple_of(i * PARTS, PARTS), PARTS), lanes] = total
                return window[:-1]

            before = tuple(
                natural[block, pl.ds(RIM - 1 - d, PARTS, stride=steps), :] for d in range(tap_count - 1)
            )
            lax.fori_loop(0, steps, tap_step, before, unroll=8)
    for block, lanes in lane_blocks(width):
        poles = [spread(row) for row in rows_of(poles_ref, lanes)]

        def state_step(i, states):
            rows = pl.ds(pl.multiple_of(i * PARTS, PARTS), PARTS)
            fresh = ks_ref[rows, lanes] * vs_ref[rows, lanes]
            return tuple(p * s + fresh for p, s in zip(poles, states))

        zero = jnp.zeros((PARTS, LANES), jnp.float32)
        states = lax.fori_loop(0, steps, state_step, (zero,) * modes, unroll=4)
        for m in range(modes):
            ends_ref[m, :, lanes] = states[m]
    part_decay = power(poles_ref[...], steps)
    own = ends_ref[:, 0, :]
    for c in range(1, PARTS):
        own = part_decay * own + ends_ref[:, c, :]
    own_ref[...] = own
    for i in range(RIM):
        first_ref[0, i : i + 1, :] = ks_ref[i * PARTS : i * PARTS + 1, :]
        first_ref[1, i : i + 1, :] = vs_ref[i * PARTS : i * PARTS + 1, :]


def long_forward(qs_ref, ks_ref, vs_ref, ends_ref, before_ref, poles_ref, residues_ref, long_ref, gated_ref, first, natural):
    tokens, width = qs_ref.shape
    modes = poles_ref.shape[0]
    steps = tokens // PARTS
    part_decay = power(poles_ref[...], steps)
    entering = before_ref[...]
    for c in range(PARTS):
        first[:, c, :] = entering
        if c < PARTS - 1:
            entering = part_decay * entering + ends_ref[:, c, :]
    for block, lanes in lane_blocks(width):
        poles = [spread(row) for row in rows_of(poles_ref, lanes)]
        residues = [spread(row) for row in rows_of(residues_ref, lanes)]

        def step(i, states):
            rows = pl.ds(pl.multiple_of(i * PARTS, PARTS), PARTS)
            fresh = ks_ref[rows, lanes] * vs_ref[rows, lanes]
            states = tuple(p * s + fresh for p, s in zip(poles, states))
            total = mixed(residues, states)
            long_ref[rows, lanes] = total
            natural[block, pl.ds(i, PARTS, stride=steps), :] = total * qs_ref[rows, lanes]
            return states

        lax.fori_loop(0, steps, step, tuple(first[m, :, lanes] for m in range(modes)), unroll=4)
    for block, lanes in lane_blocks(width):
        gated_ref[:, lanes] = natural[block].astype(gated_ref.dtype)


def mixed(residues, states):
    return added([r * s for r, s in zip(residues, states)])


def added(terms):
    while len(terms) > 1:
        terms = [a + b for a, b in zip(terms[::2], terms[1::2])] + list(terms[len(terms) // 2 * 2 :])
    return terms[0]


def back_states(kept_ref, one_up_ref, one_down_ref, three_up_ref, three_down_ref, qs_ref, long_ref, poles_ref, mixed_ref, starts_ref, own_ref, rim_ref, rim_starts, natural):
    tokens, width = qs_ref.shape
    modes = poles_ref.shape[0]
    steps = tokens // PARTS
    for block, lanes in lane_blocks(width):
        poles = [spread(row) for row in rows_of(poles_ref, lanes)]

        for half, refs in enumerate(((one_up_ref, three_up_ref), (one_down_ref, three_down_ref))):

            def add_step(n, carry):
                piece = 64
                row = pl.multiple_of(n * piece, piece)
                tile, inside = row // TILE, pl.multiple_of(row % TILE, piece)
                there = pl.ds(pl.multiple_of(half * (tokens // 2) + row, piece), piece)
                total = kept_ref[there, lanes]
                for ref in refs:
                    start = pl.multiple_of(tile * (TILE + HEAD), HEAD)
                    total = total + decoded(ref, start, pl.ds(inside, piece), lanes)
                natural[block, there, :] = total
                return carry

            lax.fori_loop(0, tokens // 128, add_step, 0)

        def step(back, states):
            i = steps - 1 - back
            rows = pl.ds(pl.multiple_of(i * PARTS, PARTS), PARTS)
            here = natural[block, pl.ds(i, PARTS, stride=steps), :]
            mixed_ref[rows, lanes] = here
            fresh = here * qs_ref[rows, lanes]
            return tuple(p * s + fresh for p, s in zip(poles, states))

        zero = jnp.zeros((PARTS, LANES), jnp.float32)
        states = lax.fori_loop(0, steps - RIM, step, (zero,) * modes, unroll=4)
        for m in range(modes):
            rim_starts[m, :, lanes] = states[m]
        states = lax.fori_loop(steps - RIM, steps, step, states, unroll=4)
        for m in range(modes):
            starts_ref[m, :, lanes] = states[m]
    part_decay = power(poles_ref[...], steps)
    own = starts_ref[:, PARTS - 1, :]
    for c in range(PARTS - 2, 0, -1):
        own = part_decay * own + starts_ref[:, c, :]
    own_ref[...] = part_decay * own + starts_ref[:, 0, :]
    rim_ref[0:modes, :] = power(poles_ref[...], steps - RIM) * own + rim_starts[:, 0, :]
    for i in range(RIM):
        here = mixed_ref[i * PARTS : i * PARTS + 1, :]
        rim_ref[modes + i : modes + i + 1, :] = here * qs_ref[i * PARTS : i * PARTS + 1, :]
        rim_ref[modes + RIM + i : modes + RIM + i + 1, :] = here * long_ref[i * PARTS : i * PARTS + 1, :]


def back_local(mixed_ref, qs_ref, poles_ref, residues_ref, local_ref):
    tokens, width = qs_ref.shape
    modes = poles_ref.shape[0]
    steps = tokens // PARTS
    for block, lanes in lane_blocks(width):
        poles = [spread(row) for row in rows_of(poles_ref, lanes)]
        residues = [spread(row) for row in rows_of(residues_ref, lanes)]

        def step(back, states):
            i = steps - 1 - back
            rows = pl.ds(pl.multiple_of(i * PARTS, PARTS), PARTS)
            fresh = mixed_ref[rows, lanes] * qs_ref[rows, lanes]
            states = tuple(p * s + fresh for p, s in zip(poles, states))
            local_ref[rows, lanes] = mixed(residues, states)
            return states

        zero = jnp.zeros((PARTS, LANES), jnp.float32)
        lax.fori_loop(0, steps, step, (zero,) * modes, unroll=4)


def short_back(value, rim, taps_ref, which, target, natural):
    tokens, width = target.shape
    tap_count = taps_ref.shape[1]
    steps = tokens // PARTS
    bottom = lax.broadcasted_iota(jnp.int32, (PARTS, LANES), 0) == PARTS - 1
    for block, lanes in lane_blocks(width):
        taps = [spread(taps_ref[which, j : j + 1, lanes]) for j in range(tap_count)]

        def tap_step(back, window):
            i = steps - 1 - back
            window = (value(pl.ds(pl.multiple_of(i * PARTS, PARTS), PARTS), lanes),) + window
            total = taps[0] * window[0]
            for j in range(1, tap_count):
                total = total + taps[j] * window[j]
            natural[block, pl.ds(i, PARTS, stride=steps), :] = total
            return window[:-1]

        after = tuple(
            jnp.where(
                bottom,
                spread(rim(d, lanes)),
                pltpu.roll(value(pl.ds(d * PARTS, PARTS), lanes), PARTS - 1, 0),
            )
            for d in range(tap_count - 1)
        )
        lax.fori_loop(0, steps, tap_step, after, unroll=8)
    for block, lanes in lane_blocks(width):
        target[:, lanes] = natural[block].astype(target.dtype)


def back_query(mixed_ref, long_ref, next_ref, taps_ref, gq_ref, natural):
    first = next_ref.shape[0] - RIM
    short_back(
        lambda rows, lanes: mixed_ref[rows, lanes] * long_ref[rows, lanes],
        lambda d, lanes: next_ref[first + d : first + d + 1, lanes],
        taps_ref, 0, gq_ref, natural,
    )


def back_filters(local_ref, ks_ref, vs_ref, starts_ref, next_ref, beyond_ref, next_kv_ref, taps_ref, poles_ref, residues_ref, gk_ref, gv_ref, last, product, natural, rims):
    tokens, width = ks_ref.shape
    modes = poles_ref.shape[0]
    steps = tokens // PARTS
    poles_all = poles_ref[...]
    residues_all = residues_ref[...]
    entering = next_ref[0:modes, :] + power(poles_all, tokens - RIM) * beyond_ref[...]
    for i in range(RIM - 1, -1, -1):
        entering = poles_all * entering + next_ref[modes + i : modes + i + 1, :]
        here = jnp.sum(residues_all * entering, axis=0, keepdims=True)
        rims[0, i : i + 1, :] = here * next_kv_ref[1, i : i + 1, :]
        rims[1, i : i + 1, :] = here * next_kv_ref[0, i : i + 1, :]
    part_decay = power(poles_all, steps)
    for c in range(PARTS - 1, -1, -1):
        last[:, c, :] = residues_all * entering
        if c:
            entering = part_decay * entering + starts_ref[:, c, :]
    for block, lanes in lane_blocks(width):
        poles = [spread(row) for row in rows_of(poles_ref, lanes)]

        def step(back, fading):
            i = steps - 1 - back
            rows = pl.ds(pl.multiple_of(i * PARTS, PARTS), PARTS)
            fading = tuple(p * s for p, s in zip(poles, fading))
            product[rows, lanes] = local_ref[rows, lanes] + added(fading)
            return fading

        lax.fori_loop(0, steps, step, tuple(last[m, :, lanes] for m in range(modes)), unroll=4)
    for which, other, target in ((1, vs_ref, gk_ref), (2, ks_ref, gv_ref)):
        short_back(
            lambda rows, lanes: product[rows, lanes] * other[rows, lanes],
            lambda d, lanes: rims[which - 1, d : d + 1, lanes],
            taps_ref, which, target, natural,
        )


def pick_shares(place_ref, weight_ref, up_ref, down_ref, arrived):
    rows = weight_ref.shape[0] // 2
    blocks = arrived.shape[2]
    depth = up_ref.shape[1]
    width = depth // blocks
    count = weight_ref.shape[1] // depth
    first = pl.multiple_of(place_ref[2] * rows, rows)
    copies = []
    for side, (message_ref, step) in enumerate(((up_ref, 1), (down_ref, count - 1))):
        for part, (x, begin, size, target) in enumerate(
            (
                (lax.rem(place_ref[0] + step, count), 0, rows, 0),
                (lax.rem(place_ref[0] + 2, count), side * (rows // 2), rows // 2, rows),
            )
        ):
            for z in range(blocks):
                column = pl.multiple_of((z * count + x) * width, width)
                copies.append(
                    pltpu.make_async_copy(
                        weight_ref.at[pl.ds(first + begin, size), pl.ds(column, width)],
                        message_ref.at[pl.ds(target, size), pl.ds(z * width, width)],
                        arrived.at[side, part, z],
                    )
                )
    for copy in copies:
        copy.start()
    for copy in copies:
        copy.wait()


def join_shares(place_ref, share, other, weight):
    rows = share.shape[0]
    core = place_ref[2]
    weight[pl.ds(pl.multiple_of(core * rows, rows), rows), :] = share
    weight[pl.ds(pl.multiple_of((1 - core) * rows, rows), rows), :] = other


def ring_product(target_ref, ring, weight_ref, column_of, first=True):
    tokens, width = target_ref.shape
    rows = tokens // 2
    for n, refs in ring:
        for half in range(2):
            target_rows = pl.ds(half * rows, rows)
            features = refs[half][...] if len(refs) == 2 else refs[0][target_rows, :]
            term = lax.dot_general(
                features,
                weight_ref[:, pl.ds(column_of(n), width)],
                (((1,), (1,)), ((), ())),
                preferred_element_type=jnp.float32,
            )
            target_ref[target_rows, :] = term if first else target_ref[target_rows, :] + term
        first = False


def early_places(early_ref):
    count = early_ref.shape[0] + 3
    return [(n % count, (early_ref.at[n + 2],)) for n in range(-2, 3)]


def late_places(count, left_ref, right_ref, *middle):
    ring = [(3, (left_ref,)), (count - 3, (right_ref,))]
    return ring + [(count // 2, middle)] if middle else ring


def in_places(early_ref, *late_refs):
    return early_places(early_ref) + late_places(early_ref.shape[0] + 3, *late_refs)


def own_columns(place_ref, count, along_x, width):
    def column_of(n):
        block = lax.rem(place_ref[3] + n, count) * along_x + place_ref[0]
        return pl.multiple_of(block * width, width)

    return column_of


def keep_start(place_ref, weight_ref, *refs):
    *block_refs, early_ref, kept_ref, arrived = refs
    copies = [
        pltpu.make_async_copy(ref, early_ref.at[n], arrived.at[n]) for n, ref in enumerate(block_refs)
    ]
    for copy in copies:
        copy.start()
    for copy in copies:
        copy.wait()
    width = kept_ref.shape[1]
    count = early_ref.shape[0] + 3
    column_of = own_columns(place_ref, count, weight_ref.shape[1] // (count * width), width)
    ring_product(kept_ref, early_places(early_ref), weight_ref, column_of)


def keep_finish(place_ref, weight_ref, started_ref, *refs):
    *late_refs, kept_ref = refs
    width = kept_ref.shape[1]
    count = RING
    column_of = own_columns(place_ref, count, weight_ref.shape[1] // (count * width), width)
    kept_ref[...] = started_ref[...]
    ring_product(kept_ref, late_places(count, *late_refs), weight_ref, column_of, False)


def encode_tile(total, coded_ref, tile):
    largest = jnp.max(jnp.abs(total), axis=0, keepdims=True) * 1.01
    largest = jnp.maximum(largest, TINY).astype(jnp.bfloat16)
    scaled = total * (SPAN / largest.astype(jnp.float32))
    square = scaled * scaled
    fourth = square * square
    eighth = fourth * fourth
    code = jnp.where(scaled < 0, -eighth, eighth)
    start = pl.multiple_of(tile * (TILE + HEAD), HEAD)
    coded_ref[pl.ds(start, HEAD), :] = jnp.broadcast_to(largest, (HEAD, largest.shape[1]))
    coded_ref[pl.ds(start + HEAD, TILE), :] = code.astype(jnp.bfloat16)


def column_on_ring(place_ref, count, width):
    return lambda n: pl.multiple_of(lax.rem(place_ref[3] + n, count) * width, width)


def far_start(place_ref, *refs):
    *ring_refs, share_ref, other_ref, far_ref, weight = refs
    width = far_ref.shape[1]
    join_shares(place_ref, share_ref[...], other_ref[...], weight)
    column_of = column_on_ring(place_ref, weight.shape[1] // width, width)
    ring_product(far_ref, in_places(*ring_refs), weight, column_of)


def far_finish(place_ref, far_ref, middle_up_ref, middle_down_ref, share_ref, other_ref, up_ref, down_ref, weight):
    half, width = middle_up_ref.shape
    count = share_ref.shape[1] // width
    column = pl.ds(column_on_ring(place_ref, count, width)(count // 2), width)
    join_shares(place_ref, share_ref[:, column], other_ref[:, column], weight)
    for side, (features_ref, coded_ref) in enumerate(((middle_up_ref, up_ref), (middle_down_ref, down_ref))):
        for t in range(half // TILE):
            term = lax.dot_general(
                features_ref[t * TILE : (t + 1) * TILE, :],
                weight[...],
                (((1,), (1,)), ((), ())),
                preferred_element_type=jnp.float32,
            )
            row = side * half + t * TILE
            encode_tile(far_ref[row : row + TILE, :] + term, coded_ref, t)


def near_products(place_ref, *refs):
    *ring_refs, shares_ref, other_ref, next_ref, last_ref, weight = refs
    width = next_ref.shape[1]
    column_of = column_on_ring(place_ref, weight.shape[1] // width, width)
    for j, target in enumerate((next_ref, last_ref)):
        join_shares(place_ref, shares_ref[j], other_ref[j], weight)
        ring_product(target, in_places(*ring_refs), weight, column_of)


def send_half(next_ref, last_ref, next_coded_ref, last_coded_ref):
    tiles = next_ref.shape[0] // TILE
    half = tiles // 2
    for t in range(half):
        start = (half + t) * TILE
        encode_tile(next_ref[start : start + TILE, :], next_coded_ref, t)
        encode_tile(last_ref[t * TILE : (t + 1) * TILE, :], last_coded_ref, t)


def send_joined(next_ref, last_ref, up_ref, down_ref, next_coded_ref, last_coded_ref):
    tiles = next_ref.shape[0] // TILE
    half = tiles // 2
    everything = pl.ds(0, next_ref.shape[1])
    for t in range(half):
        coded = t * (TILE + HEAD)
        start = (half + t) * TILE
        after = next_ref[t * TILE : (t + 1) * TILE, :]
        before = last_ref[start : start + TILE, :]
        after = after + decoded(up_ref, coded, pl.ds(0, TILE), everything)
        before = before + decoded(down_ref, coded, pl.ds(0, TILE), everything)
        encode_tile(after, next_coded_ref, t)
        encode_tile(before, last_coded_ref, t)


def decoded(coded_ref, start, rows, lanes):
    largest = coded_ref[pl.ds(start, HEAD), lanes].astype(jnp.float32)[0:1]
    code = coded_ref[pl.ds(start + HEAD + rows.start, rows.size), lanes].astype(jnp.float32)
    size = jnp.exp2(jnp.log2(jnp.maximum(jnp.abs(code), LEAST)) * 0.125)
    value = jnp.where(code < 0, -size, size) * (largest * (1.0 / SPAN))
    return jnp.where(code == 0, 0.0, value)


def local_call(kernel, outs, scratch, operands, cost):
    whole = pl.BlockSpec(memory_space=pltpu.VMEM)
    return pl.pallas_call(
        kernel,
        out_shape=outs,
        in_specs=[whole if o.ndim > 1 else pl.BlockSpec(memory_space=pltpu.SMEM) for o in operands],
        out_specs=[whole] * len(outs),
        scratch_shapes=scratch,
        compiler_params=pltpu.CompilerParams(vmem_limit_bytes=VMEM_LIMIT),
        cost_estimate=pl.CostEstimate(flops=cost, bytes_accessed=cost // 64, transcendentals=0),
    )(*operands)


def floats(*shape):
    return jax.ShapeDtypeStruct(shape, jnp.float32)


def shift(block, axis, distance, size):
    return lax.ppermute(block, axis, [(i, (i + distance) % size) for i in range(size)])


def from_behind(block, axis, distance, size):
    return lax.ppermute(
        block, axis, [(i - distance, i) for i in range(size) if 0 <= i - distance < size]
    )


def shards(
    sizes, query_in, key_in, value_in, short_taps, modal_poles, modal_residues, out_weight, grad_out
):
    ctx_count, z_count, x_count = sizes
    tokens, width = query_in.shape
    modes = modal_poles.shape[0]
    slab = floats(tokens, width)
    rounded = jax.ShapeDtypeStruct((tokens, width), jnp.bfloat16)
    per_part = floats(modes, PARTS, width)
    state = floats(modes, width)
    slab_scratch = pltpu.VMEM((tokens, width), jnp.float32)
    natural_scratch = pltpu.VMEM((width // LANES, tokens, LANES), jnp.float32)
    part_scratch = pltpu.VMEM((modes, PARTS, width), jnp.float32)
    together = lax.optimization_barrier
    decay_1 = power(modal_poles, tokens)
    decay_2 = decay_1 * decay_1

    ctx = lax.axis_index("ctx")
    place = jnp.stack([lax.axis_index("x"), ctx // 2, ctx % 2, lax.axis_index("z")])

    right_1 = shift(grad_out, "z", 1, z_count)
    left_1 = shift(grad_out, "z", -1, z_count)
    tails = jnp.stack([a[tokens - 16 :] for a in (query_in, key_in, value_in)])
    prior = from_behind(tails, "ctx", 1, ctx_count)
    place, prior = together((place, prior))
    message = jax.ShapeDtypeStruct((width // 4 * 3, z_count * width), jnp.bfloat16)
    up, down = pl.pallas_call(
        pick_shares,
        out_shape=[message] * 2,
        in_specs=[pl.BlockSpec(memory_space=pltpu.SMEM), pl.BlockSpec(memory_space=pltpu.HBM)],
        out_specs=[pl.BlockSpec(memory_space=pltpu.VMEM)] * 2,
        scratch_shapes=[pltpu.SemaphoreType.DMA((2, 2, z_count))],
        compiler_params=pltpu.CompilerParams(vmem_limit_bytes=VMEM_LIMIT),
    )(place, out_weight)
    up = shift(up, "x", 1, x_count)
    down = shift(down, "x", -1, x_count)
    q_short, k_short, v_short, ends, own_end, first_kv = local_call(
        short_filters,
        [slab, slab, slab, per_part, state, floats(2, RIM, width)],
        [pltpu.VMEM((width // LANES, tokens + RIM, LANES), jnp.float32)],
        (query_in, key_in, value_in, prior, short_taps, modal_poles),
        tokens * width * 80,
    )
    right_2 = shift(right_1, "z", 1, z_count)
    left_2 = shift(left_1, "z", -1, z_count)
    one = from_behind(own_end, "ctx", 1, ctx_count)
    pair = own_end + decay_1 * one
    two = from_behind(pair, "ctx", 2, ctx_count)
    right_2, left_2, two, up, down = together((right_2, left_2, two, up, down))

    right_3 = shift(right_2, "z", 1, z_count)
    left_3 = shift(left_2, "z", -1, z_count)
    rows = width // 2
    far_up = shift(up[rows:], "x", 1, x_count)
    far_down = shift(down[rows:], "x", -1, x_count)
    near_shares = jnp.stack([down[:rows], up[:rows]])
    other_near = lax.ppermute(near_shares, "ctx", [(i, i ^ 1) for i in range(ctx_count)])
    four = from_behind(pair + decay_2 * two, "ctx", 4, ctx_count)
    before = one + decay_1 * two + decay_2 * decay_1 * four
    long_out, gated = local_call(
        long_forward,
        [slab, rounded],
        [part_scratch, natural_scratch],
        (q_short, k_short, v_short, ends, before, modal_poles, modal_residues),
        tokens * width * 70,
    )
    anywhere = pl.BlockSpec(memory_space=pl.ANY)
    in_vmem = pl.BlockSpec(memory_space=pltpu.VMEM)
    blocks = (right_2, right_1, grad_out, left_1, left_2)
    early, kept = pl.pallas_call(
        keep_start,
        out_shape=[jax.ShapeDtypeStruct((len(blocks), tokens, width), jnp.bfloat16), slab],
        in_specs=[pl.BlockSpec(memory_space=pltpu.SMEM), in_vmem] + [anywhere] * len(blocks),
        out_specs=[in_vmem] * 2,
        scratch_shapes=[pltpu.SemaphoreType.DMA((len(blocks),))],
        compiler_params=pltpu.CompilerParams(vmem_limit_bytes=VMEM_LIMIT),
        cost_estimate=pl.CostEstimate(
            flops=tokens * width * width * 10, bytes_accessed=tokens * width * 24, transcendentals=0
        ),
    )(place, out_weight, *blocks)
    right_3, left_3, far_up, far_down, early, kept, gated, other_near = together(
        (right_3, left_3, far_up, far_down, early, kept, gated, other_near)
    )

    middle_up = shift(right_3[: tokens // 2], "z", 1, z_count)
    middle_down = shift(left_3[tokens // 2 :], "z", -1, z_count)
    far_share = jnp.concatenate([far_up, far_down])
    other_far = lax.ppermute(far_share, "ctx", [(i, i ^ 1) for i in range(ctx_count)])

    weight_scratch = pltpu.VMEM((width, z_count * width), jnp.bfloat16)
    product_cost = tokens * width * z_count * width * 2
    half_code = jax.ShapeDtypeStruct((tokens // TILE // 2 * (TILE + HEAD), width), jnp.bfloat16)
    (far,) = local_call(
        far_start,
        [slab],
        [weight_scratch],
        (place, early, left_3, right_3, far_share, other_far),
        product_cost,
    )
    middle_up, middle_down, far = together((middle_up, middle_down, far))
    on_ring = (early, left_3, right_3, middle_up, middle_down)
    up, down = local_call(
        far_finish,
        [half_code, half_code],
        [pltpu.VMEM((width, width), jnp.bfloat16)],
        (place, far, middle_up, middle_down, far_share, other_far),
        product_cost // z_count,
    )
    up = shift(up, "x", 1, x_count)
    down = shift(down, "x", -1, x_count)
    after, last = local_call(
        near_products,
        [slab, slab],
        [weight_scratch],
        (place, *on_ring, near_shares, other_near),
        2 * product_cost,
    )
    after_2, last_1 = local_call(
        send_half, [half_code, half_code], [], (after, last), tokens * width * 16
    )
    after_2 = shift(after_2, "x", 1, x_count)
    last_1 = shift(last_1, "x", -1, x_count)
    after_1, last_2 = local_call(
        send_joined, [half_code, half_code], [], (after, last, up, down), tokens * width * 32
    )
    after_1, last_2, first_kv = together((after_1, last_2, first_kv))
    after_1 = shift(after_1, "x", 1, x_count)
    last_2 = shift(last_2, "x", -1, x_count)
    next_kv = from_behind(first_kv, "ctx", -1, ctx_count)
    (kept,) = local_call(
        keep_finish, [slab], [], (place, out_weight, kept, *on_ring[1:]), product_cost // 2
    )
    after_1, after_2, last_1, last_2, kept, next_kv = together(
        (after_1, after_2, last_1, last_2, kept, next_kv)
    )
    mixed_steps, starts, own_start, rim = local_call(
        back_states,
        [slab, per_part, state, floats(modes + 2 * RIM, width)],
        [part_scratch, natural_scratch],
        (kept, after_1, after_2, last_1, last_2, q_short, long_out, modal_poles),
        tokens * width * 40,
    )

    near = from_behind(jnp.concatenate([rim, own_start]), "ctx", -1, ctx_count)
    (local,) = local_call(
        back_local, [slab], [], (mixed_steps, q_short, modal_poles, modal_residues), tokens * width * 64
    )
    two = from_behind(own_start, "ctx", -2, ctx_count)
    near, two, local = together((near, two, local))
    rim_size = modes + 2 * RIM
    near_rim = near[:rim_size]
    triple = own_start + decay_1 * near[rim_size:] + decay_2 * two
    triple_2 = from_behind(triple, "ctx", -2, ctx_count)
    triple_5 = from_behind(triple, "ctx", -5, ctx_count)
    (grad_query,) = local_call(
        back_query,
        [rounded],
        [natural_scratch],
        (mixed_steps, long_out, near_rim, short_taps),
        tokens * width * 20,
    )
    triple_2, triple_5, grad_query = together((triple_2, triple_5, grad_query))
    beyond = triple_2 + decay_2 * decay_1 * triple_5
    grad_key, grad_value = local_call(
        back_filters,
        [rounded, rounded],
        [part_scratch, slab_scratch, natural_scratch, pltpu.VMEM((2, RIM, width), jnp.float32)],
        (
            local, k_short, v_short, starts, near_rim, beyond, next_kv,
            short_taps, modal_poles, modal_residues,
        ),
        tokens * width * 80,
    )
    return gated, grad_query, grad_key, grad_value


def solution(mesh):
    ctx_count, tp_count = mesh.shape["ctx"], mesh.shape["tp"]
    sizes = (ctx_count, tp_count // X_COUNT, X_COUNT)
    grid = Mesh(mesh.devices.reshape(sizes), ("ctx", "z", "x"))
    tp = ("z", "x")
    placed = (
        P("ctx", tp),
        P("ctx", tp),
        P("ctx", tp),
        P(None, None, tp),
        P(None, tp),
        P(None, tp),
        P(tp, None),
        P("ctx", tp),
    )
    return jax.shard_map(
        functools.partial(shards, sizes),
        mesh=grid,
        in_specs=placed,
        out_specs=(P("ctx", tp),) * 4,
        check_vma=False,
    )
```

```python
import functools
import jax
import jax.numpy as jnp
from jax import lax
from jax.experimental import pallas as pl
from jax.experimental.pallas import tpu as pltpu
from jax.sharding import Mesh, PartitionSpec as P

LANES = 128
PARTS = 8
RIM = 8
X_COUNT = 4
RING = 8
TILE = 256
HEAD = 16
SPAN = 32768.0
TINY = 1e-30
LEAST = 1e-37
VMEM_LIMIT = 16 * 1024 * 1024


def power(base, exponent):
    result = None
    while exponent:
        if exponent & 1:
            result = base if result is None else result * base
        exponent >>= 1
        if exponent:
            base = base * base
    return result


def rows_of(ref, lanes):
    return [ref[m : m + 1, lanes] for m in range(ref.shape[0])]


def spread(row):
    return jnp.broadcast_to(row, (PARTS, LANES))


def lane_blocks(width):
    return [(n, pl.ds(n * LANES, LANES)) for n in range(width // LANES)]


def short_filters(q_ref, k_ref, v_ref, prior_ref, taps_ref, poles_ref, qs_ref, ks_ref, vs_ref, ends_ref, own_ref, first_ref, natural):
    tokens, width = q_ref.shape
    tap_count = taps_ref.shape[1]
    modes = poles_ref.shape[0]
    steps = tokens // PARTS
    for which, (source, target) in enumerate(((q_ref, qs_ref), (k_ref, ks_ref), (v_ref, vs_ref))):
        for block, lanes in lane_blocks(width):
            natural[block, 0:RIM, :] = prior_ref[which, :, lanes].astype(jnp.float32)[prior_ref.shape[1] - RIM :]
            natural[block, RIM:, :] = source[:, lanes].astype(jnp.float32)
        for block, lanes in lane_blocks(width):
            taps = [spread(taps_ref[which, j : j + 1, lanes]) for j in range(tap_count)]

            def tap_step(i, window):
                fresh = natural[block, pl.ds(RIM + i, PARTS, stride=steps), :]
                window = (fresh,) + window
                total = taps[0] * window[0]
                for j in range(1, tap_count):
                    total = total + taps[j] * window[j]
                target[pl.ds(pl.multiple_of(i * PARTS, PARTS), PARTS), lanes] = total
                return window[:-1]

            before = tuple(
                natural[block, pl.ds(RIM - 1 - d, PARTS, stride=steps), :] for d in range(tap_count - 1)
            )
            lax.fori_loop(0, steps, tap_step, before, unroll=8)
    for block, lanes in lane_blocks(width):
        poles = [spread(row) for row in rows_of(poles_ref, lanes)]

        def state_step(i, states):
            rows = pl.ds(pl.multiple_of(i * PARTS, PARTS), PARTS)
            fresh = ks_ref[rows, lanes] * vs_ref[rows, lanes]
            return tuple(p * s + fresh for p, s in zip(poles, states))

        zero = jnp.zeros((PARTS, LANES), jnp.float32)
        states = lax.fori_loop(0, steps, state_step, (zero,) * modes, unroll=8)
        for m in range(modes):
            ends_ref[m, :, lanes] = states[m]
    part_decay = power(poles_ref[...], steps)
    own = ends_ref[:, 0, :]
    for c in range(1, PARTS):
        own = part_decay * own + ends_ref[:, c, :]
    own_ref[...] = own
    for i in range(RIM):
        first_ref[0, i : i + 1, :] = ks_ref[i * PARTS : i * PARTS + 1, :]
        first_ref[1, i : i + 1, :] = vs_ref[i * PARTS : i * PARTS + 1, :]


def long_forward(qs_ref, ks_ref, vs_ref, ends_ref, before_ref, poles_ref, residues_ref, long_ref, gated_ref, first, natural):
    tokens, width = qs_ref.shape
    modes = poles_ref.shape[0]
    steps = tokens // PARTS
    part_decay = power(poles_ref[...], steps)
    entering = before_ref[...]
    for c in range(PARTS):
        first[:, c, :] = entering
        if c < PARTS - 1:
            entering = part_decay * entering + ends_ref[:, c, :]
    for block, lanes in lane_blocks(width):
        poles = [spread(row) for row in rows_of(poles_ref, lanes)]
        residues = [spread(row) for row in rows_of(residues_ref, lanes)]

        def step(i, states):
            rows = pl.ds(pl.multiple_of(i * PARTS, PARTS), PARTS)
            fresh = ks_ref[rows, lanes] * vs_ref[rows, lanes]
            states = tuple(p * s + fresh for p, s in zip(poles, states))
            total = mixed(residues, states)
            long_ref[rows, lanes] = total
            natural[block, pl.ds(i, PARTS, stride=steps), :] = total * qs_ref[rows, lanes]
            return states

        lax.fori_loop(0, steps, step, tuple(first[m, :, lanes] for m in range(modes)), unroll=8)
    for block, lanes in lane_blocks(width):
        gated_ref[:, lanes] = natural[block].astype(gated_ref.dtype)


def mixed(residues, states):
    return added([r * s for r, s in zip(residues, states)])


def added(terms):
    while len(terms) > 1:
        terms = [a + b for a, b in zip(terms[::2], terms[1::2])] + list(terms[len(terms) // 2 * 2 :])
    return terms[0]


def back_states(kept_ref, one_up_ref, one_down_ref, three_up_ref, three_down_ref, qs_ref, long_ref, poles_ref, mixed_ref, starts_ref, own_ref, rim_ref, rim_starts, natural):
    tokens, width = qs_ref.shape
    modes = poles_ref.shape[0]
    steps = tokens // PARTS
    for block, lanes in lane_blocks(width):
        poles = [spread(row) for row in rows_of(poles_ref, lanes)]

        for half, refs in enumerate(((one_up_ref, three_up_ref), (one_down_ref, three_down_ref))):

            def add_step(n, carry):
                piece = 64
                row = pl.multiple_of(n * piece, piece)
                tile, inside = row // TILE, pl.multiple_of(row % TILE, piece)
                there = pl.ds(pl.multiple_of(half * (tokens // 2) + row, piece), piece)
                total = kept_ref[there, lanes]
                for ref in refs:
                    start = pl.multiple_of(tile * (TILE + HEAD), HEAD)
                    total = total + decoded(ref, start, pl.ds(inside, piece), lanes)
                natural[block, there, :] = total
                return carry

            lax.fori_loop(0, tokens // 128, add_step, 0)

        def step(back, states):
            i = steps - 1 - back
            rows = pl.ds(pl.multiple_of(i * PARTS, PARTS), PARTS)
            here = natural[block, pl.ds(i, PARTS, stride=steps), :]
            mixed_ref[rows, lanes] = here
            fresh = here * qs_ref[rows, lanes]
            return tuple(p * s + fresh for p, s in zip(poles, states))

        zero = jnp.zeros((PARTS, LANES), jnp.float32)
        states = lax.fori_loop(0, steps - RIM, step, (zero,) * modes, unroll=8)
        for m in range(modes):
            rim_starts[m, :, lanes] = states[m]
        states = lax.fori_loop(steps - RIM, steps, step, states, unroll=8)
        for m in range(modes):
            starts_ref[m, :, lanes] = states[m]
    part_decay = power(poles_ref[...], steps)
    own = starts_ref[:, PARTS - 1, :]
    for c in range(PARTS - 2, 0, -1):
        own = part_decay * own + starts_ref[:, c, :]
    own_ref[...] = part_decay * own + starts_ref[:, 0, :]
    rim_ref[0:modes, :] = power(poles_ref[...], steps - RIM) * own + rim_starts[:, 0, :]
    for i in range(RIM):
        here = mixed_ref[i * PARTS : i * PARTS + 1, :]
        rim_ref[modes + i : modes + i + 1, :] = here * qs_ref[i * PARTS : i * PARTS + 1, :]
        rim_ref[modes + RIM + i : modes + RIM + i + 1, :] = here * long_ref[i * PARTS : i * PARTS + 1, :]


def back_local(mixed_ref, qs_ref, poles_ref, residues_ref, local_ref):
    tokens, width = qs_ref.shape
    modes = poles_ref.shape[0]
    steps = tokens // PARTS
    for block, lanes in lane_blocks(width):
        poles = [spread(row) for row in rows_of(poles_ref, lanes)]
        residues = [spread(row) for row in rows_of(residues_ref, lanes)]

        def step(back, states):
            i = steps - 1 - back
            rows = pl.ds(pl.multiple_of(i * PARTS, PARTS), PARTS)
            fresh = mixed_ref[rows, lanes] * qs_ref[rows, lanes]
            states = tuple(p * s + fresh for p, s in zip(poles, states))
            local_ref[rows, lanes] = mixed(residues, states)
            return states

        zero = jnp.zeros((PARTS, LANES), jnp.float32)
        lax.fori_loop(0, steps, step, (zero,) * modes, unroll=8)


def short_back(value, rim, taps_ref, which, target, natural):
    tokens, width = target.shape
    tap_count = taps_ref.shape[1]
    steps = tokens // PARTS
    bottom = lax.broadcasted_iota(jnp.int32, (PARTS, LANES), 0) == PARTS - 1
    for block, lanes in lane_blocks(width):
        taps = [spread(taps_ref[which, j : j + 1, lanes]) for j in range(tap_count)]

        def tap_step(back, window):
            i = steps - 1 - back
            window = (value(pl.ds(pl.multiple_of(i * PARTS, PARTS), PARTS), lanes),) + window
            total = taps[0] * window[0]
            for j in range(1, tap_count):
                total = total + taps[j] * window[j]
            natural[block, pl.ds(i, PARTS, stride=steps), :] = total
            return window[:-1]

        after = tuple(
            jnp.where(
                bottom,
                spread(rim(d, lanes)),
                pltpu.roll(value(pl.ds(d * PARTS, PARTS), lanes), PARTS - 1, 0),
            )
            for d in range(tap_count - 1)
        )
        lax.fori_loop(0, steps, tap_step, after, unroll=8)
    for block, lanes in lane_blocks(width):
        target[:, lanes] = natural[block].astype(target.dtype)


def back_query(mixed_ref, long_ref, next_ref, taps_ref, gq_ref, natural):
    first = next_ref.shape[0] - RIM
    short_back(
        lambda rows, lanes: mixed_ref[rows, lanes] * long_ref[rows, lanes],
        lambda d, lanes: next_ref[first + d : first + d + 1, lanes],
        taps_ref, 0, gq_ref, natural,
    )


def back_filters(local_ref, ks_ref, vs_ref, starts_ref, next_ref, beyond_ref, next_kv_ref, taps_ref, poles_ref, residues_ref, gk_ref, gv_ref, last, product, natural, rims):
    tokens, width = ks_ref.shape
    modes = poles_ref.shape[0]
    steps = tokens // PARTS
    poles_all = poles_ref[...]
    residues_all = residues_ref[...]
    entering = next_ref[0:modes, :] + power(poles_all, tokens - RIM) * beyond_ref[...]
    for i in range(RIM - 1, -1, -1):
        entering = poles_all * entering + next_ref[modes + i : modes + i + 1, :]
        here = jnp.sum(residues_all * entering, axis=0, keepdims=True)
        rims[0, i : i + 1, :] = here * next_kv_ref[1, i : i + 1, :]
        rims[1, i : i + 1, :] = here * next_kv_ref[0, i : i + 1, :]
    part_decay = power(poles_all, steps)
    for c in range(PARTS - 1, -1, -1):
        last[:, c, :] = residues_all * entering
        if c:
            entering = part_decay * entering + starts_ref[:, c, :]
    for block, lanes in lane_blocks(width):
        poles = [spread(row) for row in rows_of(poles_ref, lanes)]

        def step(back, fading):
            i = steps - 1 - back
            rows = pl.ds(pl.multiple_of(i * PARTS, PARTS), PARTS)
            fading = tuple(p * s for p, s in zip(poles, fading))
            product[rows, lanes] = local_ref[rows, lanes] + added(fading)
            return fading

        lax.fori_loop(0, steps, step, tuple(last[m, :, lanes] for m in range(modes)), unroll=8)
    for which, other, target in ((1, vs_ref, gk_ref), (2, ks_ref, gv_ref)):
        short_back(
            lambda rows, lanes: product[rows, lanes] * other[rows, lanes],
            lambda d, lanes: rims[which - 1, d : d + 1, lanes],
            taps_ref, which, target, natural,
        )


def pick_shares(place_ref, weight_ref, up_ref, down_ref, arrived):
    rows = weight_ref.shape[0] // 2
    blocks = arrived.shape[2]
    depth = up_ref.shape[1]
    width = depth // blocks
    count = weight_ref.shape[1] // depth
    first = pl.multiple_of(place_ref[2] * rows, rows)
    copies = []
    for side, (message_ref, step) in enumerate(((up_ref, 1), (down_ref, count - 1))):
        for part, (x, begin, size, target) in enumerate(
            (
                (lax.rem(place_ref[0] + step, count), 0, rows, 0),
                (lax.rem(place_ref[0] + 2, count), side * (rows // 2), rows // 2, rows),
            )
        ):
            for z in range(blocks):
                column = pl.multiple_of((z * count + x) * width, width)
                copies.append(
                    pltpu.make_async_copy(
                        weight_ref.at[pl.ds(first + begin, size), pl.ds(column, width)],
                        message_ref.at[pl.ds(target, size), pl.ds(z * width, width)],
                        arrived.at[side, part, z],
                    )
                )
    for copy in copies:
        copy.start()
    for copy in copies:
        copy.wait()


def join_shares(place_ref, share, other, weight):
    rows = share.shape[0]
    core = place_ref[2]
    weight[pl.ds(pl.multiple_of(core * rows, rows), rows), :] = share
    weight[pl.ds(pl.multiple_of((1 - core) * rows, rows), rows), :] = other


def ring_product(target_ref, ring, weight_ref, column_of, first=True):
    tokens, width = target_ref.shape
    rows = tokens // 2
    for n, refs in ring:
        for half in range(2):
            target_rows = pl.ds(half * rows, rows)
            features = refs[half][...] if len(refs) == 2 else refs[0][target_rows, :]
            term = lax.dot_general(
                features,
                weight_ref[:, pl.ds(column_of(n), width)],
                (((1,), (1,)), ((), ())),
                preferred_element_type=jnp.float32,
            )
            target_ref[target_rows, :] = term if first else target_ref[target_rows, :] + term
        first = False


def early_places(early_ref):
    count = early_ref.shape[0] + 3
    return [(n % count, (early_ref.at[n + 2],)) for n in range(-2, 3)]


def late_places(count, left_ref, right_ref, *middle):
    ring = [(3, (left_ref,)), (count - 3, (right_ref,))]
    return ring + [(count // 2, middle)] if middle else ring


def in_places(early_ref, *late_refs):
    return early_places(early_ref) + late_places(early_ref.shape[0] + 3, *late_refs)


def own_columns(place_ref, count, along_x, width):
    def column_of(n):
        block = lax.rem(place_ref[3] + n, count) * along_x + place_ref[0]
        return pl.multiple_of(block * width, width)

    return column_of


def keep_start(place_ref, weight_ref, *refs):
    *block_refs, early_ref, kept_ref, arrived = refs
    copies = [
        pltpu.make_async_copy(ref, early_ref.at[n], arrived.at[n]) for n, ref in enumerate(block_refs)
    ]
    for copy in copies:
        copy.start()
    for copy in copies:
        copy.wait()
    width = kept_ref.shape[1]
    count = early_ref.shape[0] + 3
    column_of = own_columns(place_ref, count, weight_ref.shape[1] // (count * width), width)
    ring_product(kept_ref, early_places(early_ref), weight_ref, column_of)


def keep_finish(place_ref, weight_ref, started_ref, *refs):
    *late_refs, kept_ref = refs
    width = kept_ref.shape[1]
    count = RING
    column_of = own_columns(place_ref, count, weight_ref.shape[1] // (count * width), width)
    kept_ref[...] = started_ref[...]
    ring_product(kept_ref, late_places(count, *late_refs), weight_ref, column_of, False)


def encode_tile(total, coded_ref, tile):
    largest = jnp.max(jnp.abs(total), axis=0, keepdims=True) * 1.01
    largest = jnp.maximum(largest, TINY).astype(jnp.bfloat16)
    scaled = total * (SPAN / largest.astype(jnp.float32))
    square = scaled * scaled
    fourth = square * square
    eighth = fourth * fourth
    code = jnp.where(scaled < 0, -eighth, eighth)
    start = pl.multiple_of(tile * (TILE + HEAD), HEAD)
    coded_ref[pl.ds(start, HEAD), :] = jnp.broadcast_to(largest, (HEAD, largest.shape[1]))
    coded_ref[pl.ds(start + HEAD, TILE), :] = code.astype(jnp.bfloat16)


def column_on_ring(place_ref, count, width):
    return lambda n: pl.multiple_of(lax.rem(place_ref[3] + n, count) * width, width)


def far_start(place_ref, *refs):
    *ring_refs, share_ref, other_ref, far_ref, weight = refs
    width = far_ref.shape[1]
    join_shares(place_ref, share_ref[...], other_ref[...], weight)
    column_of = column_on_ring(place_ref, weight.shape[1] // width, width)
    ring_product(far_ref, in_places(*ring_refs), weight, column_of)


def far_finish(place_ref, far_ref, middle_up_ref, middle_down_ref, share_ref, other_ref, up_ref, down_ref, weight):
    half, width = middle_up_ref.shape
    count = share_ref.shape[1] // width
    column = pl.ds(column_on_ring(place_ref, count, width)(count // 2), width)
    join_shares(place_ref, share_ref[:, column], other_ref[:, column], weight)
    for side, (features_ref, coded_ref) in enumerate(((middle_up_ref, up_ref), (middle_down_ref, down_ref))):
        for t in range(half // TILE):
            term = lax.dot_general(
                features_ref[t * TILE : (t + 1) * TILE, :],
                weight[...],
                (((1,), (1,)), ((), ())),
                preferred_element_type=jnp.float32,
            )
            row = side * half + t * TILE
            encode_tile(far_ref[row : row + TILE, :] + term, coded_ref, t)


def near_products(place_ref, *refs):
    *ring_refs, shares_ref, other_ref, next_ref, last_ref, weight = refs
    width = next_ref.shape[1]
    column_of = column_on_ring(place_ref, weight.shape[1] // width, width)
    for j, target in enumerate((next_ref, last_ref)):
        join_shares(place_ref, shares_ref[j], other_ref[j], weight)
        ring_product(target, in_places(*ring_refs), weight, column_of)


def send_half(next_ref, last_ref, next_coded_ref, last_coded_ref):
    tiles = next_ref.shape[0] // TILE
    half = tiles // 2
    for t in range(half):
        start = (half + t) * TILE
        encode_tile(next_ref[start : start + TILE, :], next_coded_ref, t)
        encode_tile(last_ref[t * TILE : (t + 1) * TILE, :], last_coded_ref, t)


def send_joined(next_ref, last_ref, up_ref, down_ref, next_coded_ref, last_coded_ref):
    tiles = next_ref.shape[0] // TILE
    half = tiles // 2
    everything = pl.ds(0, next_ref.shape[1])
    for t in range(half):
        coded = t * (TILE + HEAD)
        start = (half + t) * TILE
        after = next_ref[t * TILE : (t + 1) * TILE, :]
        before = last_ref[start : start + TILE, :]
        after = after + decoded(up_ref, coded, pl.ds(0, TILE), everything)
        before = before + decoded(down_ref, coded, pl.ds(0, TILE), everything)
        encode_tile(after, next_coded_ref, t)
        encode_tile(before, last_coded_ref, t)


def decoded(coded_ref, start, rows, lanes):
    largest = coded_ref[pl.ds(start, HEAD), lanes].astype(jnp.float32)[0:1]
    code = coded_ref[pl.ds(start + HEAD + rows.start, rows.size), lanes].astype(jnp.float32)
    size = jnp.exp2(jnp.log2(jnp.maximum(jnp.abs(code), LEAST)) * 0.125)
    value = jnp.where(code < 0, -size, size) * (largest * (1.0 / SPAN))
    return jnp.where(code == 0, 0.0, value)


def local_call(kernel, outs, scratch, operands, cost):
    whole = pl.BlockSpec(memory_space=pltpu.VMEM)
    return pl.pallas_call(
        kernel,
        out_shape=outs,
        in_specs=[whole if o.ndim > 1 else pl.BlockSpec(memory_space=pltpu.SMEM) for o in operands],
        out_specs=[whole] * len(outs),
        scratch_shapes=scratch,
        compiler_params=pltpu.CompilerParams(vmem_limit_bytes=VMEM_LIMIT),
        cost_estimate=pl.CostEstimate(flops=cost, bytes_accessed=cost // 64, transcendentals=0),
    )(*operands)


def floats(*shape):
    return jax.ShapeDtypeStruct(shape, jnp.float32)


def shift(block, axis, distance, size):
    return lax.ppermute(block, axis, [(i, (i + distance) % size) for i in range(size)])


def from_behind(block, axis, distance, size):
    return lax.ppermute(
        block, axis, [(i - distance, i) for i in range(size) if 0 <= i - distance < size]
    )


def shards(
    sizes, query_in, key_in, value_in, short_taps, modal_poles, modal_residues, out_weight, grad_out
):
    ctx_count, z_count, x_count = sizes
    tokens, width = query_in.shape
    modes = modal_poles.shape[0]
    slab = floats(tokens, width)
    rounded = jax.ShapeDtypeStruct((tokens, width), jnp.bfloat16)
    per_part = floats(modes, PARTS, width)
    state = floats(modes, width)
    slab_scratch = pltpu.VMEM((tokens, width), jnp.float32)
    natural_scratch = pltpu.VMEM((width // LANES, tokens, LANES), jnp.float32)
    part_scratch = pltpu.VMEM((modes, PARTS, width), jnp.float32)
    together = lax.optimization_barrier
    decay_1 = power(modal_poles, tokens)
    decay_2 = decay_1 * decay_1

    ctx = lax.axis_index("ctx")
    place = jnp.stack([lax.axis_index("x"), ctx // 2, ctx % 2, lax.axis_index("z")])

    right_1 = shift(grad_out, "z", 1, z_count)
    left_1 = shift(grad_out, "z", -1, z_count)
    tails = jnp.stack([a[tokens - 16 :] for a in (query_in, key_in, value_in)])
    prior = from_behind(tails, "ctx", 1, ctx_count)
    place, prior = together((place, prior))
    message = jax.ShapeDtypeStruct((width // 4 * 3, z_count * width), jnp.bfloat16)
    up, down = pl.pallas_call(
        pick_shares,
        out_shape=[message] * 2,
        in_specs=[pl.BlockSpec(memory_space=pltpu.SMEM), pl.BlockSpec(memory_space=pltpu.HBM)],
        out_specs=[pl.BlockSpec(memory_space=pltpu.VMEM)] * 2,
        scratch_shapes=[pltpu.SemaphoreType.DMA((2, 2, z_count))],
        compiler_params=pltpu.CompilerParams(vmem_limit_bytes=VMEM_LIMIT),
    )(place, out_weight)
    up = shift(up, "x", 1, x_count)
    down = shift(down, "x", -1, x_count)
    q_short, k_short, v_short, ends, own_end, first_kv = local_call(
        short_filters,
        [slab, slab, slab, per_part, state, floats(2, RIM, width)],
        [pltpu.VMEM((width // LANES, tokens + RIM, LANES), jnp.float32)],
        (query_in, key_in, value_in, prior, short_taps, modal_poles),
        tokens * width * 80,
    )
    right_2 = shift(right_1, "z", 1, z_count)
    left_2 = shift(left_1, "z", -1, z_count)
    one = from_behind(own_end, "ctx", 1, ctx_count)
    pair = own_end + decay_1 * one
    two = from_behind(pair, "ctx", 2, ctx_count)
    right_2, left_2, two, up, down = together((right_2, left_2, two, up, down))

    right_3 = shift(right_2, "z", 1, z_count)
    left_3 = shift(left_2, "z", -1, z_count)
    rows = width // 2
    far_up = shift(up[rows:], "x", 1, x_count)
    far_down = shift(down[rows:], "x", -1, x_count)
    near_shares = jnp.stack([down[:rows], up[:rows]])
    other_near = lax.ppermute(near_shares, "ctx", [(i, i ^ 1) for i in range(ctx_count)])
    four = from_behind(pair + decay_2 * two, "ctx", 4, ctx_count)
    before = one + decay_1 * two + decay_2 * decay_1 * four
    long_out, gated = local_call(
        long_forward,
        [slab, rounded],
        [part_scratch, natural_scratch],
        (q_short, k_short, v_short, ends, before, modal_poles, modal_residues),
        tokens * width * 70,
    )
    anywhere = pl.BlockSpec(memory_space=pl.ANY)
    in_vmem = pl.BlockSpec(memory_space=pltpu.VMEM)
    blocks = (right_2, right_1, grad_out, left_1, left_2)
    early, kept = pl.pallas_call(
        keep_start,
        out_shape=[jax.ShapeDtypeStruct((len(blocks), tokens, width), jnp.bfloat16), slab],
        in_specs=[pl.BlockSpec(memory_space=pltpu.SMEM), in_vmem] + [anywhere] * len(blocks),
        out_specs=[in_vmem] * 2,
        scratch_shapes=[pltpu.SemaphoreType.DMA((len(blocks),))],
        compiler_params=pltpu.CompilerParams(vmem_limit_bytes=VMEM_LIMIT),
        cost_estimate=pl.CostEstimate(
            flops=tokens * width * width * 10, bytes_accessed=tokens * width * 24, transcendentals=0
        ),
    )(place, out_weight, *blocks)
    right_3, left_3, far_up, far_down, early, kept, gated, other_near = together(
        (right_3, left_3, far_up, far_down, early, kept, gated, other_near)
    )

    middle_up = shift(right_3[: tokens // 2], "z", 1, z_count)
    middle_down = shift(left_3[tokens // 2 :], "z", -1, z_count)
    far_share = jnp.concatenate([far_up, far_down])
    other_far = lax.ppermute(far_share, "ctx", [(i, i ^ 1) for i in range(ctx_count)])

    weight_scratch = pltpu.VMEM((width, z_count * width), jnp.bfloat16)
    product_cost = tokens * width * z_count * width * 2
    half_code = jax.ShapeDtypeStruct((tokens // TILE // 2 * (TILE + HEAD), width), jnp.bfloat16)
    (far,) = local_call(
        far_start,
        [slab],
        [weight_scratch],
        (place, early, left_3, right_3, far_share, other_far),
        product_cost,
    )
    middle_up, middle_down, far = together((middle_up, middle_down, far))
    on_ring = (early, left_3, right_3, middle_up, middle_down)
    up, down = local_call(
        far_finish,
        [half_code, half_code],
        [pltpu.VMEM((width, width), jnp.bfloat16)],
        (place, far, middle_up, middle_down, far_share, other_far),
        product_cost // z_count,
    )
    up = shift(up, "x", 1, x_count)
    down = shift(down, "x", -1, x_count)
    after, last = local_call(
        near_products,
        [slab, slab],
        [weight_scratch],
        (place, *on_ring, near_shares, other_near),
        2 * product_cost,
    )
    after_2, last_1 = local_call(
        send_half, [half_code, half_code], [], (after, last), tokens * width * 16
    )
    after_2 = shift(after_2, "x", 1, x_count)
    last_1 = shift(last_1, "x", -1, x_count)
    after_1, last_2 = local_call(
        send_joined, [half_code, half_code], [], (after, last, up, down), tokens * width * 32
    )
    after_1, last_2, first_kv = together((after_1, last_2, first_kv))
    after_1 = shift(after_1, "x", 1, x_count)
    last_2 = shift(last_2, "x", -1, x_count)
    next_kv = from_behind(first_kv, "ctx", -1, ctx_count)
    (kept,) = local_call(
        keep_finish, [slab], [], (place, out_weight, kept, *on_ring[1:]), product_cost // 2
    )
    after_1, after_2, last_1, last_2, kept, next_kv = together(
        (after_1, after_2, last_1, last_2, kept, next_kv)
    )
    mixed_steps, starts, own_start, rim = local_call(
        back_states,
        [slab, per_part, state, floats(modes + 2 * RIM, width)],
        [part_scratch, natural_scratch],
        (kept, after_1, after_2, last_1, last_2, q_short, long_out, modal_poles),
        tokens * width * 40,
    )

    near = from_behind(jnp.concatenate([rim, own_start]), "ctx", -1, ctx_count)
    (local,) = local_call(
        back_local, [slab], [], (mixed_steps, q_short, modal_poles, modal_residues), tokens * width * 64
    )
    two = from_behind(own_start, "ctx", -2, ctx_count)
    near, two, local = together((near, two, local))
    rim_size = modes + 2 * RIM
    near_rim = near[:rim_size]
    triple = own_start + decay_1 * near[rim_size:] + decay_2 * two
    triple_2 = from_behind(triple, "ctx", -2, ctx_count)
    triple_5 = from_behind(triple, "ctx", -5, ctx_count)
    (grad_query,) = local_call(
        back_query,
        [rounded],
        [natural_scratch],
        (mixed_steps, long_out, near_rim, short_taps),
        tokens * width * 20,
    )
    triple_2, triple_5, grad_query = together((triple_2, triple_5, grad_query))
    beyond = triple_2 + decay_2 * decay_1 * triple_5
    grad_key, grad_value = local_call(
        back_filters,
        [rounded, rounded],
        [part_scratch, slab_scratch, natural_scratch, pltpu.VMEM((2, RIM, width), jnp.float32)],
        (
            local, k_short, v_short, starts, near_rim, beyond, next_kv,
            short_taps, modal_poles, modal_residues,
        ),
        tokens * width * 80,
    )
    return gated, grad_query, grad_key, grad_value


def solution(mesh):
    ctx_count, tp_count = mesh.shape["ctx"], mesh.shape["tp"]
    sizes = (ctx_count, tp_count // X_COUNT, X_COUNT)
    grid = Mesh(mesh.devices.reshape(sizes), ("ctx", "z", "x"))
    tp = ("z", "x")
    placed = (
        P("ctx", tp),
        P("ctx", tp),
        P("ctx", tp),
        P(None, None, tp),
        P(None, tp),
        P(None, tp),
        P(tp, None),
        P("ctx", tp),
    )
    return jax.shard_map(
        functools.partial(shards, sizes),
        mesh=grid,
        in_specs=placed,
        out_specs=(P("ctx", tp),) * 4,
        check_vma=False,
    )
```
